128 devices in a mesh: dp: 16 (over y, z_lo, core), tensor: 8 (over z_hi, x).
Axes of the slice: x: 4, y: 4, z: 4 (z_hi: 2, z_lo: 2; z = z_hi * 2 + z_lo), core: 2. Of those that a mesh axis runs over, the one named last changes fastest.
Arguments:
- layer_input: bfloat16 [16384, 1024], P(('dp', 'tensor')), may hold values from -6 to 6
- cotangent: bfloat16 [16384, 1024], P(('dp', 'tensor')), may hold values from -6 to 6
- segment: int32 [16384], P('dp'), may hold values from 0 to 2, as said below
- live_mask: int32 [16384], P('dp'), may hold values from 0 to 1, as said below
- query_weight: bfloat16 [2, 1024, 1024], P(None, 'dp', 'tensor'), may hold values from -0.1875 to 0.1875
- key_weight: bfloat16 [2, 1024, 1024], P(None, 'dp', 'tensor'), may hold values from -0.1875 to 0.1875
- value_weight: bfloat16 [2, 1024, 1024], P(None, 'dp', 'tensor'), may hold values from -0.1875 to 0.1875
- out_weight: bfloat16 [2, 1024, 1024], P(None, 'tensor', 'dp'), may hold values from -3 to 3
- up_weight: bfloat16 [2, 1024, 4096], P(None, 'dp', 'tensor'), may hold values from -0.1875 to 0.1875
- down_weight: bfloat16 [2, 4096, 1024], P(None, 'tensor', 'dp'), may hold values from -0.09375 to 0.09375
- query_bias: float32 [2, 1024], P(None, 'tensor'), may hold values from -3 to 3
- value_bias: float32 [2, 1024], P(None, 'tensor'), may hold values from -3 to 3
- up_bias: float32 [2, 4096], P(None, 'tensor'), may hold values from -3 to 3
- out_bias: float32 [2, 1024], replicated, may hold values from -3 to 3
- down_bias: float32 [2, 1024], replicated, may hold values from -3 to 3
- attention_gain: float32 [2, 1024], replicated, may hold values from 0.5 to 1.5
- attention_shift: float32 [2, 1024], replicated, may hold values from -3 to 3
- output_gain: float32 [2, 1024], replicated, may hold values from 0.5 to 1.5
- output_shift: float32 [2, 1024], replicated, may hold values from -3 to 3
Outputs:
- layer_output: float32 [16384, 1024], P(('dp', 'tensor'))
- input_grad: float32 [16384, 1024], P(('dp', 'tensor'))
- query_weight_grad: float32 [2, 1024, 1024], P(None, 'dp', 'tensor')
- key_weight_grad: float32 [2, 1024, 1024], P(None, 'dp', 'tensor')
- value_weight_grad: float32 [2, 1024, 1024], P(None, 'dp', 'tensor')
- out_weight_grad: float32 [2, 1024, 1024], P(None, 'tensor', 'dp')
- up_weight_grad: float32 [2, 1024, 4096], P(None, 'dp', 'tensor')
- down_weight_grad: float32 [2, 4096, 1024], P(None, 'tensor', 'dp')
- query_bias_grad: float32 [2, 1024], P(None, 'tensor')
- value_bias_grad: float32 [2, 1024], P(None, 'tensor')
- up_bias_grad: float32 [2, 4096], P(None, 'tensor')
- out_bias_grad: float32 [2, 1024], replicated
- down_bias_grad: float32 [2, 1024], replicated
- attention_gain_grad: float32 [2, 1024], replicated
- attention_shift_grad: float32 [2, 1024], replicated
- output_gain_grad: float32 [2, 1024], replicated
- output_shift_grad: float32 [2, 1024], replicated
The draws below stay inside these ranges and needn't reach their ends.
Inputs may be any that keep to these rules, and one draw needn't show every extreme that they name: Within each aligned block of 1024 positions the segment numbers are 0, 1, 2 in that order, never falling, each present. `live_mask`: within each segment the ones form a prefix of one or more positions.
All inputs are finite; a program needn't handle non-finite values.
Results may differ from the reference program's by a relative error of at most 0.039.
Values may be sent and summed in bfloat16 or wider, within the bound.
No kernel may reach another device: no remote copies, remote signals or barrier semaphores. Data moves between devices by JAX's collectives and lax.ppermute only.
A program may use at most 128 MiB of HBM per device.

```python
import jax
import jax.numpy as jnp
from jax import lax

D = 1024
FF = 4096
HEADS = 16
HEAD_DIM = 64
LAYERS = 2
TOK_DEV = 128
GROUP = 1024
TOKENS = 16384


def layout_tables(key):
    seeded = jax.random.fold_in(key, 911)
    split_keys = jax.random.split(seeded, 5)
    groups = TOKENS // GROUP
    quarter = TOK_DEV // 4
    half_dev = TOK_DEV // 2
    lead_size = jax.random.randint(split_keys[0], (groups,), 1, half_dev + 1)
    tail_size = jax.random.randint(split_keys[1], (groups,), 1, half_dev + 1)
    middle_size = GROUP - lead_size - tail_size
    lead_live = jax.random.randint(split_keys[2], (groups,), 1, lead_size + 1)
    middle_live = jax.random.randint(split_keys[3], (groups,), middle_size - quarter, middle_size + 1)
    tail_live = jax.random.randint(split_keys[4], (groups,), 1, tail_size + 1)
    position = jnp.arange(GROUP, dtype=jnp.int32)[None, :]
    tail_start = GROUP - tail_size
    segment_ids = (position >= lead_size[:, None]).astype(jnp.int32) + (position >= tail_start[:, None]).astype(jnp.int32)
    begin_at = jnp.where(segment_ids == 0, 0, jnp.where(segment_ids == 1, lead_size[:, None], tail_start[:, None]))
    live_count = jnp.where(segment_ids == 0, lead_live[:, None], jnp.where(segment_ids == 1, middle_live[:, None], tail_live[:, None]))
    is_live = (position - begin_at < live_count).astype(jnp.int32)
    return (segment_ids.reshape(TOKENS), is_live.reshape(TOKENS))


def draw_segment(key, part):
    return layout_tables(key)[0]


def draw_live_mask(key, part):
    return layout_tables(key)[1]


def block_scale(stream_key, dims, cuts, least, largest):
    factor_of = 1.0
    for dim, shards_of in cuts:
        heights = jax.random.uniform(jax.random.fold_in(jax.random.fold_in(stream_key, 6), dim), (shards_of,), jnp.float32, least / len(cuts), largest / len(cuts))
        factor_of = factor_of * jnp.repeat(jnp.exp(heights), dims[dim] // shards_of).reshape((-1,) + (1,) * (len(dims) - 1 - dim))
    return factor_of


def normal_values(own_key, shape, scale, reach, cuts=(), kind=jnp.bfloat16):
    drawn = jax.random.normal(own_key, shape, jnp.float32) * scale
    if len(cuts) > 0:
        drawn = block_scale(own_key, shape, cuts, -0.22, 0.18) * drawn
    return jnp.clip(drawn, min=-reach, max=reach).astype(kind)


def setup_inputs(seed: int = 0) -> dict:
    seeds = jax.random.split(jax.random.key(seed), 20)
    return {
        "layer_input": normal_values(seeds[0], (TOKENS, D), 1.0, 6.0, ((0, 128),)),
        "cotangent": normal_values(seeds[1], (TOKENS, D), 1.0, 6.0, ((0, 128),)),
        "segment": draw_segment(jax.random.fold_in(seeds[19], 71), 0),
        "live_mask": draw_live_mask(jax.random.fold_in(seeds[19], 71), 0),
        "query_weight": normal_values(seeds[4], (LAYERS, D, D), D ** -0.5, 0.1875, ((1, 16), (2, 8))),
        "key_weight": normal_values(seeds[5], (LAYERS, D, D), D ** -0.5, 0.1875, ((1, 16), (2, 8))),
        "value_weight": normal_values(seeds[6], (LAYERS, D, D), D ** -0.5, 0.1875, ((1, 16), (2, 8))),
        "out_weight": normal_values(seeds[7], (LAYERS, D, D), (max(D // 256, 2)) ** -0.5, 3.0, ((1, 8), (2, 16))),
        "up_weight": normal_values(seeds[8], (LAYERS, D, FF), D ** -0.5, 0.1875, ((1, 16), (2, 8))),
        "down_weight": normal_values(seeds[9], (LAYERS, FF, D), FF ** -0.5, 0.09375, ((1, 8), (2, 16))),
        "query_bias": normal_values(seeds[10], (LAYERS, D), 0.5, 3.0, ((1, 8),), jnp.float32),
        "value_bias": normal_values(seeds[11], (LAYERS, D), 0.5, 3.0, ((1, 8),), jnp.float32),
        "up_bias": normal_values(seeds[12], (LAYERS, FF), 0.5, 3.0, ((1, 8),), jnp.float32),
        "out_bias": normal_values(seeds[13], (LAYERS, D), 0.5, 3.0, (), jnp.float32),
        "down_bias": normal_values(seeds[14], (LAYERS, D), 0.5, 3.0, (), jnp.float32),
        "attention_gain": jnp.clip(1.0 + 0.1 * jax.random.normal(seeds[15], (LAYERS, D), jnp.float32), 0.5, 1.5),
        "attention_shift": normal_values(seeds[16], (LAYERS, D), 0.5, 3.0, (), jnp.float32),
        "output_gain": jnp.clip(1.0 + 0.1 * jax.random.normal(seeds[17], (LAYERS, D), jnp.float32), 0.5, 1.5),
        "output_shift": normal_values(seeds[18], (LAYERS, D), 0.5, 3.0, (), jnp.float32),
    }


NORM_EPS = 1e-12
MASKED = -1000000000.0

@jax.custom_vjp
def low(v):
    return lax.optimization_barrier(v.astype(jnp.bfloat16)).astype(jnp.float32)

@jax.custom_vjp
def low_back(v):
    return v

def low_keep(v):
    return (low(v), None)

def low_pass(kept, grad):
    return (grad,)

def back_keep(v):
    return (v, None)

def back_low(kept, grad):
    return (low(grad),)
low.defvjp(low_keep, low_pass)
low_back.defvjp(back_keep, back_low)

def normalize(rows, gain, shift):
    center = rows - lax.optimization_barrier(jnp.mean(rows, axis=-1, keepdims=True))
    spread = lax.optimization_barrier(jnp.mean(center * center, axis=-1, keepdims=True))
    return center * lax.rsqrt(spread + NORM_EPS) * gain + shift

def project(left, right):
    return jnp.dot(left, right, precision=lax.Precision.HIGHEST)

def attend_group(pieces):
    queries, key_rows, value_rows, segment_ids, live_ids = pieces
    scores = jnp.einsum('qhd,khd->hqk', queries, key_rows, precision=lax.Precision.HIGHEST) * HEAD_DIM ** (-0.5)
    scores = low_back(scores)
    allowed = (segment_ids[:, None] == segment_ids[None, :]) & (live_ids[None, :] == 1)
    scores = jnp.where(allowed[None], scores, MASKED)
    row_max = lax.optimization_barrier(jnp.max(scores, axis=-1, keepdims=True))
    exp_scores = jnp.exp(scores - row_max)
    soft = exp_scores / lax.optimization_barrier(jnp.sum(exp_scores, axis=-1, keepdims=True))
    soft = low(low_back(soft))
    return jnp.einsum('hqk,khd->qhd', soft, value_rows, precision=lax.Precision.HIGHEST)

def encoder_layer(current, layer, segment, live_mask, params):
    query_weight, key_weight, value_weight, out_weight, up_weight, down_weight, query_bias, value_bias, up_bias, out_bias, down_bias, attention_gain, attention_shift, output_gain, output_shift = params
    group_count = TOKENS // GROUP
    gathered = low(current)
    queries = low(low_back(project(gathered, query_weight[layer]) + query_bias[layer]))
    key_rows = low(low_back(project(gathered, key_weight[layer])))
    value_rows = low(low_back(project(gathered, value_weight[layer]) + value_bias[layer]))
    shape_heads = (group_count, GROUP, HEADS, HEAD_DIM)
    attended = lax.map(jax.checkpoint(attend_group), (queries.reshape(shape_heads), key_rows.reshape(shape_heads), value_rows.reshape(shape_heads), segment.reshape(group_count, GROUP), live_mask.reshape(group_count, GROUP)))
    attended = low(low_back(attended.reshape(TOKENS, D)))
    first_sum = current + low_back(project(attended, out_weight[layer]) + out_bias[layer])
    normed_mid = normalize(first_sum, attention_gain[layer], attention_shift[layer])
    mid_low = low(normed_mid)
    pre_gelu = low_back(project(mid_low, up_weight[layer]) + up_bias[layer])
    activated = low(jax.nn.gelu(pre_gelu, approximate=False))
    second_sum = normed_mid + low_back(project(activated, down_weight[layer]) + down_bias[layer])
    return normalize(second_sum, output_gain[layer], output_shift[layer])

def reference(layer_input, cotangent, segment, live_mask, query_weight, key_weight, value_weight, out_weight, up_weight, down_weight, query_bias, value_bias, up_bias, out_bias, down_bias, attention_gain, attention_shift, output_gain, output_shift):
    params = tuple((item.astype(jnp.float32) for item in (query_weight, key_weight, value_weight, out_weight, up_weight, down_weight, query_bias, value_bias, up_bias, out_bias, down_bias, attention_gain, attention_shift, output_gain, output_shift)))

    def forward(inputs, *weights):
        current = inputs
        for layer in range(LAYERS):
            current = encoder_layer(current, layer, segment, live_mask, weights)
        return current
    result, backward = jax.vjp(forward, layer_input.astype(jnp.float32), *params)
    grads = backward(cotangent.astype(jnp.float32))
    return (result, grads[0], grads[1], grads[2], grads[3], grads[4], grads[5], grads[6], grads[7], grads[8], grads[9], grads[10], grads[11], grads[12], grads[13], grads[14], grads[15])
```

```python
import jax
import jax.numpy as jnp
from jax import lax
from jax.sharding import Mesh, PartitionSpec as P

HEAD_DIM = 64
NORM_EPS = 1e-12
MASKED = -1000000000.0
F32 = jnp.float32
BF16 = jnp.bfloat16

AXES = ("y", "zl", "c", "zh", "x")
DP = ("y", "zl", "c")
TENSOR = ("zh", "x")
OWNERS = ("y", "zl", "zh")
HOPS = (0, 1, 3, 2)
ORDER = (2, 1, 3, 0)


def dot(left, right, left_dim, right_dim):
    return lax.dot_general(
        left, right, (((left_dim,), (right_dim,)), ((), ())), preferred_element_type=F32
    )


def along_x(value, hop):
    ring = lax.axis_size("x")
    return lax.ppermute(value, "x", [(i, (i + hop) % ring) for i in range(ring)])


def other_core(value):
    return lax.ppermute(value, "c", [(0, 1), (1, 0)])


def swap_core_z(value):
    ring = lax.axis_size("x")
    pairs = []
    for core in range(2):
        for high in range(2):
            for x in range(ring):
                pairs.append(((core * 2 + high) * ring + x, (high * 2 + core) * ring + x))
    return lax.ppermute(value, ("c", "zh", "x"), pairs)


def gather_pairs(rows):
    chunks = {}
    for hop in (1, 3, 2, 0):
        mine = along_x(rows, hop) if hop else rows
        chunks[hop] = jnp.concatenate([mine, other_core(mine)], axis=0)
    return chunks


def scatter_pairs(parts):
    total = None
    for hop in ORDER:
        part = parts[hop]
        half = part.shape[0] // 2
        both = part[:half] + other_core(part[half:].astype(BF16)).astype(F32)
        if hop:
            both = along_x(both.astype(BF16), -hop).astype(F32)
        total = both if total is None else total + both
    return total


def normalized(rows):
    center = rows - jnp.mean(rows, axis=-1, keepdims=True)
    spread = jnp.mean(center * center, axis=-1, keepdims=True)
    scale = lax.rsqrt(spread + NORM_EPS)
    return center * scale, scale


def norm_back(grad, unit, scale, gain):
    gain_grad = jnp.sum(grad * unit, axis=0)
    shift_grad = jnp.sum(grad, axis=0)
    scaled = grad * gain
    mean_all = jnp.mean(scaled, axis=-1, keepdims=True)
    mean_unit = jnp.mean(scaled * unit, axis=-1, keepdims=True)
    return scale * (scaled - mean_all - unit * mean_unit), gain_grad, shift_grad


def gelu_exact(values):
    return jax.nn.gelu(values, approximate=False)


def attend(queries, keys, values, allowed):
    mixed, kept = [], []
    for head in range(queries.shape[1] // HEAD_DIM):
        cols = slice(head * HEAD_DIM, (head + 1) * HEAD_DIM)
        scores = dot(queries[:, cols], keys[:, cols], 1, 1) * HEAD_DIM**-0.5
        scores = jnp.where(allowed, scores, MASKED)
        exps = jnp.exp(scores - jnp.max(scores, axis=-1, keepdims=True))
        soft = (exps / jnp.sum(exps, axis=-1, keepdims=True)).astype(BF16)
        kept.append(soft)
        mixed.append(dot(soft, values[:, cols], 1, 0).astype(BF16))
    return jnp.concatenate(mixed, axis=1), kept


def attend_chunk_back(queries, keys, values, kept, grads):
    grad_q, grad_k, grad_v = [], [], []
    for head in range(queries.shape[1] // HEAD_DIM):
        cols = slice(head * HEAD_DIM, (head + 1) * HEAD_DIM)
        soft = kept[head]
        wide = soft.astype(F32)
        grad_soft = dot(grads[:, cols], values[:, cols], 1, 1).astype(BF16).astype(F32)
        row = jnp.sum(grad_soft * wide, axis=-1, keepdims=True)
        grad_scores = (wide * (grad_soft - row)).astype(BF16)
        grad_q.append(dot(grad_scores, keys[:, cols], 1, 0) * HEAD_DIM**-0.5)
        grad_k.append(dot(grad_scores, queries[:, cols], 0, 0))
        grad_v.append(dot(soft, grads[:, cols], 0, 0))
    return (
        jnp.concatenate(grad_q, axis=1).astype(BF16),
        jnp.concatenate(grad_k, axis=1),
        jnp.concatenate(grad_v, axis=1),
    )


def stack_chunks(chunks):
    return jnp.concatenate([chunks[hop] for hop in HOPS], axis=0)


def on_device(
    layer_input,
    cotangent,
    segment,
    live_mask,
    query_weight,
    key_weight,
    value_weight,
    out_weight,
    up_weight,
    down_weight,
    query_bias,
    value_bias,
    up_bias,
    out_bias,
    down_bias,
    attention_gain,
    attention_shift,
    output_gain,
    output_shift,
):
    layers = query_weight.shape[0]
    core, high, x = lax.axis_index("c"), lax.axis_index("zh"), lax.axis_index("x")
    ring = lax.axis_size("x")
    owners = 16
    rows_in = swap_core_z(layer_input)

    attn_shards = jnp.concatenate(
        [query_weight, key_weight, value_weight, jnp.swapaxes(out_weight, 1, 2)], axis=2
    )
    ffn_shards = jnp.concatenate([up_weight, jnp.swapaxes(down_weight, 1, 2)], axis=2)
    shard_rows, attn_cols = attn_shards.shape[1:]
    ffn_cols = ffn_shards.shape[2]
    width = shard_rows * owners
    attn_shards = swap_core_z(attn_shards)
    ffn_shards = swap_core_z(ffn_shards)
    first = jnp.broadcast_to(attn_shards[0], (owners, shard_rows, attn_cols))
    attn_mats = [lax.all_to_all(first, OWNERS, 0, 0, tiled=True).reshape(width, attn_cols)]
    ffn_mats = [lax.all_gather(ffn_shards[0], OWNERS, axis=0, tiled=True)]
    for layer in range(1, layers):
        attn_mats.append(lax.all_gather(attn_shards[layer], OWNERS, axis=0, tiled=True))
        ffn_mats.append(lax.all_gather(ffn_shards[layer], OWNERS, axis=0, tiled=True))
    qkv_cols = 3 * attn_cols // 4
    head_cols = attn_cols // 4
    ffn_half = ffn_cols // 2

    biases = jnp.concatenate([query_bias, value_bias, up_bias], axis=1)
    biases = swap_core_z(biases)
    query_bias = biases[:, :head_cols]
    value_bias = biases[:, head_cols : 2 * head_cols]
    up_bias = biases[:, 2 * head_cols :]

    packed = (segment * 2 + live_mask).astype(F32)
    packed = jnp.where(core == high, packed, other_core(packed)).reshape(2, ring, -1)
    packed = jnp.where(core == 0, packed, packed[::-1])
    ordered = []
    for hop in HOPS:
        ordered.append(lax.dynamic_index_in_dim(packed, lax.rem(x + ring - hop, ring), 1, False))
    marks = jnp.stack(ordered).reshape(len(HOPS), -1)
    seg_chunks = jnp.floor(marks * 0.5)
    live = (marks - 2 * seg_chunks).reshape(-1)
    key_mark = jnp.where(live > 0.5, seg_chunks.reshape(-1), -1.0)
    allowed = {
        hop: seg_chunks[index][:, None] == key_mark[None, :] for index, hop in enumerate(HOPS)
    }

    current = rows_in.astype(F32)
    saved = []
    for layer in range(layers):
        qkv_mat = attn_mats[layer][:, :qkv_cols]
        out_mat = attn_mats[layer][:, qkv_cols:]
        up_mat = ffn_mats[layer][:, :ffn_half]
        down_mat = ffn_mats[layer][:, ffn_half:]
        qkv_bias = jnp.concatenate(
            [query_bias[layer], jnp.zeros_like(query_bias[layer]), value_bias[layer]]
        )
        inputs = gather_pairs(current.astype(BF16))
        qkv = {hop: (dot(inputs[hop], qkv_mat, 1, 0) + qkv_bias).astype(BF16) for hop in HOPS}
        keys = stack_chunks({hop: qkv[hop][:, head_cols : 2 * head_cols] for hop in HOPS})
        values = stack_chunks({hop: qkv[hop][:, 2 * head_cols :] for hop in HOPS})
        attended, soft, parts = {}, {}, {}
        for hop in ORDER:
            attended[hop], soft[hop] = attend(
                qkv[hop][:, :head_cols], keys, values, allowed[hop]
            )
            parts[hop] = dot(attended[hop], out_mat, 1, 1)
        first_sum = current + scatter_pairs(parts) + out_bias[layer]
        mid_unit, mid_scale = normalized(first_sum)
        normed_mid = mid_unit * attention_gain[layer] + attention_shift[layer]
        mids = gather_pairs(normed_mid.astype(BF16))
        pre_gelu, activated, parts = {}, {}, {}
        for hop in ORDER:
            pre_gelu[hop] = dot(mids[hop], up_mat, 1, 0) + up_bias[layer]
            activated[hop] = gelu_exact(pre_gelu[hop]).astype(BF16)
            parts[hop] = dot(activated[hop], down_mat, 1, 1)
        second_sum = normed_mid + scatter_pairs(parts) + down_bias[layer]
        out_unit, out_scale = normalized(second_sum)
        current = out_unit * output_gain[layer] + output_shift[layer]
        saved.append(
            (inputs, qkv, keys, values, attended, soft, mid_unit, mid_scale, mids, pre_gelu,
             activated, out_unit, out_scale)
        )
    layer_output = swap_core_z(current.astype(BF16)).astype(F32)

    grad_rows = swap_core_z(cotangent).astype(F32)
    attn_grads, ffn_grads = [None] * layers, [None] * layers
    head_sums, row_sums = [None] * layers, [None] * layers
    tail = None
    for layer in reversed(range(layers)):
        (inputs, qkv, keys, values, attended, soft, mid_unit, mid_scale, mids, pre_gelu,
         activated, out_unit, out_scale) = saved[layer]
        qkv_mat = attn_mats[layer][:, :qkv_cols]
        out_mat = attn_mats[layer][:, qkv_cols:]
        up_mat = ffn_mats[layer][:, :ffn_half]
        down_mat = ffn_mats[layer][:, ffn_half:]
        grad_second, out_gain_term, out_shift_term = norm_back(
            grad_rows, out_unit, out_scale, output_gain[layer]
        )
        branch_low = grad_second.astype(BF16)
        down_bias_term = jnp.sum(branch_low.astype(F32), axis=0)
        branch = gather_pairs(branch_low)
        grad_pre, parts = {}, {}
        for hop in ORDER:
            grad_act = dot(branch[hop], down_mat, 1, 0)
            grad_pre[hop] = jax.vjp(gelu_exact, pre_gelu[hop])[1](grad_act)[0].astype(BF16)
            parts[hop] = dot(grad_pre[hop], up_mat, 1, 1)
        grad_mid = grad_second + scatter_pairs(parts)
        all_pre = stack_chunks(grad_pre)
        up_bias_term = jnp.sum(all_pre.astype(F32), axis=0)
        up_grad = dot(stack_chunks(mids), all_pre, 0, 0)
        down_grad = dot(stack_chunks(branch), stack_chunks(activated), 0, 0)
        terms = jnp.concatenate([up_grad.astype(BF16), down_grad.astype(BF16)], axis=1)
        ffn_grads[layer] = lax.psum_scatter(terms, OWNERS, scatter_dimension=0, tiled=True).astype(F32)

        grad_first, att_gain_term, att_shift_term = norm_back(
            grad_mid, mid_unit, mid_scale, attention_gain[layer]
        )
        attn_low = grad_first.astype(BF16)
        out_bias_term = jnp.sum(attn_low.astype(F32), axis=0)
        attn_chunks = gather_pairs(attn_low)
        grad_q, grad_k, grad_v = {}, [], []
        for hop in ORDER:
            grad_att = dot(attn_chunks[hop], out_mat, 1, 0).astype(BF16)
            q_rows = qkv[hop][:, :head_cols]
            grad_q[hop], k_term, v_term = attend_chunk_back(
                q_rows, keys, values, soft[hop], grad_att
            )
            grad_k.append(k_term)
            grad_v.append(v_term)
        grad_keys = (sum(grad_k) * HEAD_DIM**-0.5).astype(BF16)
        grad_values = sum(grad_v).astype(BF16)
        grad_qkv = jnp.concatenate([stack_chunks(grad_q), grad_keys, grad_values], axis=1)
        count = grad_qkv.shape[0] // len(HOPS)
        parts = {}
        for index, hop in enumerate(HOPS):
            parts[hop] = dot(grad_qkv[index * count : (index + 1) * count], qkv_mat, 1, 1)
        grad_rows = grad_first + scatter_pairs(parts)
        qkv_grad = dot(stack_chunks(inputs), grad_qkv, 0, 0)
        out_grad = dot(stack_chunks(attn_chunks), stack_chunks(attended), 0, 0)
        terms = jnp.concatenate([qkv_grad.astype(BF16), out_grad.astype(BF16)], axis=1)
        bias_terms = jnp.sum(grad_qkv.astype(F32), axis=0)
        head_sums[layer] = jnp.concatenate(
            [bias_terms[:head_cols], bias_terms[2 * head_cols :], up_bias_term]
        )
        row_sums[layer] = jnp.stack(
            [out_bias_term, down_bias_term, att_gain_term, att_shift_term, out_gain_term,
             out_shift_term]
        )
        if layer > 0:
            attn_grads[layer] = lax.psum_scatter(terms, OWNERS, scatter_dimension=0, tiled=True).astype(F32)
        else:
            tail = terms

    slices = jnp.stack(row_sums).reshape(layers * 6, 2, ring, -1)
    slices = jnp.transpose(slices, (1, 2, 0, 3))
    mine = lax.dynamic_index_in_dim(slices, core, 0, False)
    send = lax.dynamic_index_in_dim(slices, 1 - core, 0, False)
    both = mine + other_core(send)
    kept = None
    for hop in HOPS:
        part = lax.dynamic_index_in_dim(both, lax.rem(x + ring - hop, ring), 0, False)
        part = along_x(part, -hop) if hop else part
        kept = part if kept is None else kept + part
    small = jnp.concatenate([jnp.stack(head_sums).reshape(-1), kept.reshape(-1)])
    small_len = small.shape[0]
    extra = -(-small_len // (16 * attn_cols)) * 16
    small_rows = jnp.pad(small, (0, extra * attn_cols - small_len)).reshape(1, extra, attn_cols)
    sent = jnp.concatenate(
        [
            tail.reshape(owners, shard_rows, attn_cols),
            jnp.broadcast_to(small_rows.astype(BF16), (owners, extra, attn_cols)),
        ],
        axis=1,
    )
    got = lax.all_to_all(sent, OWNERS, 0, 0, tiled=True)
    got = jnp.sum(got.astype(F32), axis=0)
    attn_grads[0] = got[:shard_rows]
    small = got[shard_rows:].reshape(-1)[:small_len]
    head_len = layers * head_sums[0].shape[0]

    grad_all = jnp.concatenate([jnp.stack(attn_grads), jnp.stack(ffn_grads)], axis=2)
    grad_all = swap_core_z(grad_all.astype(BF16)).astype(F32)
    bias_all = swap_core_z(small[:head_len].reshape(layers, -1))
    input_grad = swap_core_z(grad_rows.astype(BF16)).astype(F32)

    piece = small[head_len:].reshape(layers * 6, -1)
    table = jnp.zeros((2, ring) + piece.shape, F32)
    for hop in HOPS:
        one = along_x(piece, hop) if hop else piece
        where = lax.rem(x + ring - hop, ring)
        table = lax.dynamic_update_slice(table, one[None, None], (core, where, 0, 0))
    pair = lax.dynamic_slice_in_dim(table, core, 1, 0)
    table = lax.dynamic_update_slice(table, other_core(pair), (1 - core, 0, 0, 0))
    rows_out = jnp.transpose(table, (2, 0, 1, 3)).reshape(layers, 6, -1)

    def cols(start, count):
        return grad_all[:, :, start : start + count]

    return (
        layer_output,
        input_grad,
        cols(0, head_cols),
        cols(head_cols, head_cols),
        cols(2 * head_cols, head_cols),
        jnp.swapaxes(cols(3 * head_cols, head_cols), 1, 2),
        cols(attn_cols, ffn_half),
        jnp.swapaxes(cols(attn_cols + ffn_half, ffn_half), 1, 2),
        bias_all[:, :head_cols],
        bias_all[:, head_cols : 2 * head_cols],
        bias_all[:, 2 * head_cols :],
        rows_out[:, 0],
        rows_out[:, 1],
        rows_out[:, 2],
        rows_out[:, 3],
        rows_out[:, 4],
        rows_out[:, 5],
    )


def solution(mesh):
    split = Mesh(mesh.devices.reshape(4, 2, 2, 2, 4), AXES)
    rows = P(DP + TENSOR, None)
    tall = P(None, DP, TENSOR)
    wide = P(None, TENSOR, DP)
    held = P(None, TENSOR)
    return jax.shard_map(
        on_device,
        mesh=split,
        in_specs=(rows, rows, P(DP), P(DP), tall, tall, tall, wide, tall, wide, held, held, held)
        + (P(),) * 6,
        out_specs=(rows, rows, tall, tall, tall, wide, tall, wide, held, held, held) + (P(),) * 6,
        check_vma=False,
    )
```

```python
import jax
import jax.numpy as jnp
from jax import lax
from jax.experimental import pallas as pl
from jax.experimental.pallas import tpu as pltpu
from jax.sharding import Mesh, PartitionSpec as P

HEAD_DIM = 64
NORM_EPS = 1e-12
MASKED = -1000000000.0
F32 = jnp.float32
BF16 = jnp.bfloat16

AXES = ("y", "zl", "c", "zh", "x")
DP = ("y", "zl", "c")
TENSOR = ("zh", "x")
OWNERS = ("y", "zl", "zh")
HOPS = (0, 1, 3, 2)
ORDER = (2, 1, 3, 0)
ARRIVAL = (0, 1, 3, 2)


def dot(left, right, left_dim, right_dim):
    return lax.dot_general(
        left, right, (((left_dim,), (right_dim,)), ((), ())), preferred_element_type=F32
    )


def along_x(value, hop):
    ring = lax.axis_size("x")
    return lax.ppermute(value, "x", [(i, (i + hop) % ring) for i in range(ring)])


def other_core(value):
    return lax.ppermute(value, "c", [(0, 1), (1, 0)])


def swap_core_z(value):
    ring = lax.axis_size("x")
    pairs = []
    for core in range(2):
        for high in range(2):
            for x in range(ring):
                pairs.append(((core * 2 + high) * ring + x, (high * 2 + core) * ring + x))
    return lax.ppermute(value, ("c", "zh", "x"), pairs)


def gather_pairs(rows):
    mine = {hop: along_x(rows, hop) if hop else rows for hop in (1, 3, 2, 0)}
    return {hop: (mine[hop], other_core(mine[hop])) for hop in ARRIVAL}


def scatter_pairs(parts):
    total = None
    for hop in ORDER:
        keep, send = parts[hop]
        both = keep + other_core(send).astype(F32)
        if hop:
            both = along_x(both.astype(BF16), -hop).astype(F32)
        total = both if total is None else total + both
    return total


def normalized(rows):
    center = rows - jnp.mean(rows, axis=-1, keepdims=True)
    spread = jnp.mean(center * center, axis=-1, keepdims=True)
    scale = lax.rsqrt(spread + NORM_EPS)
    return center * scale, scale


def norm_back(grad, unit, scale, gain):
    gain_grad = jnp.sum(grad * unit, axis=0)
    shift_grad = jnp.sum(grad, axis=0)
    scaled = grad * gain
    mean_all = jnp.mean(scaled, axis=-1, keepdims=True)
    mean_unit = jnp.mean(scaled * unit, axis=-1, keepdims=True)
    return scale * (scaled - mean_all - unit * mean_unit), gain_grad, shift_grad


def whole(array):
    rank = len(array.shape)
    return pl.BlockSpec(array.shape, lambda *_: (0,) * rank)


def call(body, args, outs, flops, grid=(), in_specs=None, out_specs=None):
    size = sum(a.size * a.dtype.itemsize for a in (*args, *outs))
    return pl.pallas_call(
        body,
        grid=grid,
        in_specs=in_specs or [whole(a) for a in args],
        out_specs=out_specs or [whole(o) for o in outs],
        out_shape=list(outs),
        compiler_params=pltpu.CompilerParams(vmem_limit_bytes=40 * 1024 * 1024),
        cost_estimate=pl.CostEstimate(flops=flops, bytes_accessed=size, transcendentals=0),
    )(*args)


def shaped(shape, dtype):
    return jax.ShapeDtypeStruct(shape, dtype)


def both_rows(mine, other):
    return jnp.concatenate([mine[...], other[...]], axis=0)


def store_part(part, keep, send):
    half = keep.shape[0]
    keep[...] = part[:half]
    send[...] = part[half:].astype(BF16)


def part_shapes(rows, width):
    return [shaped((rows, width), F32), shaped((rows, width), BF16)]


def qkv_body(mine, other, mat, bias, query, key, value):
    out = (dot(both_rows(mine, other), mat[...], 1, 0) + bias[...]).astype(BF16)
    step = query.shape[1]
    query[...] = out[:, :step]
    key[...] = out[:, step : 2 * step]
    value[...] = out[:, 2 * step :]


def make_qkv(pair, mat, bias):
    rows, width = pair[0].shape
    out = shaped((2 * rows, mat.shape[1] // 3), BF16)
    return call(qkv_body, (*pair, mat, bias), [out] * 3, 4 * rows * mat.size)


def lanes_of(shape, head):
    return lax.broadcasted_iota(jnp.int32, shape, 1) // HEAD_DIM == head


def attend_body(query, key, value, row_mark, key_mark, out_mat, mixed, soft, keep, send):
    allowed = row_mark[...] == key_mark[...]
    total = jnp.zeros(query.shape, F32)
    for head in range(soft.shape[0]):
        lanes = lanes_of(query.shape, head)
        chosen = jnp.where(lanes, query[...], jnp.zeros(query.shape, BF16))
        scores = dot(chosen, key[...], 1, 1) * HEAD_DIM**-0.5
        scores = jnp.where(allowed, scores, MASKED)
        exps = jnp.exp(scores - jnp.max(scores, axis=-1, keepdims=True))
        probs = (exps * (1.0 / jnp.sum(exps, axis=-1, keepdims=True))).astype(BF16)
        soft[head] = probs
        total = jnp.where(lanes, dot(probs, value[...], 1, 0), total)
    low = total.astype(BF16)
    mixed[...] = low
    store_part(dot(low, out_mat[...], 1, 1), keep, send)


def attend(query, key, value, row_mark, key_mark, out_mat):
    rows, width = query.shape
    heads = width // HEAD_DIM
    outs = [shaped((rows, width), BF16), shaped((heads, rows, key.shape[0]), BF16)]
    outs += part_shapes(rows // 2, out_mat.shape[0])
    flops = 4 * heads * rows * key.size + 2 * rows * out_mat.size
    return call(attend_body, (query, key, value, row_mark, key_mark, out_mat), outs, 3 * flops)


def attend_back_body(mine, other, out_mat, query, key, value, soft, key_in, value_in, grad_query, key_out, value_out):
    grads = dot(both_rows(mine, other), out_mat[...], 1, 0).astype(BF16)
    for_query = jnp.zeros(query.shape, F32)
    for_key = jnp.zeros(key.shape, F32)
    for_value = jnp.zeros(key.shape, F32)
    for head in range(soft.shape[0]):
        lanes = lanes_of(query.shape, head)
        tall = lanes_of(key.shape, head)
        probs = soft[head]
        wide = probs.astype(F32)
        chosen = jnp.where(lanes, grads, jnp.zeros(query.shape, BF16))
        grad_soft = dot(chosen, value[...], 1, 1)
        row = jnp.sum(grad_soft * wide, axis=-1, keepdims=True)
        scores = (wide * (grad_soft - row)).astype(BF16)
        for_query = jnp.where(lanes, dot(scores, key[...], 1, 0), for_query)
        for_key = jnp.where(tall, dot(scores, query[...], 0, 0), for_key)
        for_value = jnp.where(tall, dot(probs, grads, 0, 0), for_value)
    grad_query[...] = (for_query * HEAD_DIM**-0.5).astype(BF16)
    key_out[...] = key_in[...] + for_key * HEAD_DIM**-0.5
    value_out[...] = value_in[...] + for_value


def attend_back(pair, out_mat, query, key, value, soft, key_sum, value_sum):
    outs = [shaped(query.shape, BF16), shaped(key.shape, F32), shaped(key.shape, F32)]
    args = (*pair, out_mat, query, key, value, soft, key_sum, value_sum)
    flops = 8 * soft.shape[0] * query.shape[0] * key.size
    return call(attend_back_body, args, outs, 2 * flops)


def inputs_back_body(grad_query, grad_key, grad_value, mat, joined, sums, keep, send):
    rows = jnp.concatenate(
        [grad_query[...], grad_key[...].astype(BF16), grad_value[...].astype(BF16)], axis=1
    )
    joined[...] = rows
    sums[...] = jnp.sum(rows.astype(F32), axis=0, keepdims=True)
    store_part(dot(rows, mat[...], 1, 1), keep, send)


def inputs_back(grad_query, grad_key, grad_value, index, mat):
    rows, width = grad_query.shape
    outs = [shaped((rows, 3 * width), BF16), shaped((1, 3 * width), F32)]
    outs += part_shapes(rows // 2, mat.shape[0])
    block = pl.BlockSpec((rows, width), lambda *_: (index, 0))
    args = (grad_query, grad_key, grad_value, mat)
    specs = [whole(grad_query), block, block, whole(mat)]
    return call(inputs_back_body, args, outs, 2 * rows * mat.size, (1,), specs)


def ffn_body(mine, other, up, bias, down, act, slope, keep, send):
    pre = dot(both_rows(mine, other), up[...], 1, 0) + bias[...]
    area = 0.5 + 0.5 * lax.erf(pre * 0.7071067811865476)
    low = (pre * area).astype(BF16)
    act[...] = low
    slope[...] = (area + pre * (jnp.exp(pre * pre * -0.5) * 0.3989422804014327)).astype(BF16)
    store_part(dot(low, down[...], 1, 1), keep, send)


def ffn(pair, up, bias, down):
    rows, width = pair[0].shape
    outs = [shaped((2 * rows, up.shape[1]), BF16)] * 2 + part_shapes(rows, width)
    return call(ffn_body, (*pair, up, bias, down), outs, 4 * rows * (up.size + down.size))


def ffn_back_body(mine, other, up, down, slope, grad, sums, keep, send):
    low = (dot(both_rows(mine, other), down[...], 1, 0) * slope[...].astype(F32)).astype(BF16)
    grad[...] = low
    sums[...] = jnp.sum(low.astype(F32), axis=0, keepdims=True)
    store_part(dot(low, up[...], 1, 1), keep, send)


def ffn_back(pair, up, down, slope):
    rows, width = pair[0].shape
    outs = [shaped(slope.shape, BF16), shaped((1, slope.shape[1]), F32)] + part_shapes(rows, width)
    return call(ffn_back_body, (*pair, up, down, slope), outs, 4 * rows * (up.size + down.size))


def weight_body(count, *refs):
    out = refs[-1]
    start = 0
    for side in range(2):
        here = refs[side * 3 * count : (side + 1) * 3 * count]
        left = jnp.concatenate([ref[...] for ref in here[: 2 * count]], axis=0)
        right = jnp.concatenate([ref[...] for ref in here[2 * count :]], axis=0)
        out[:, start : start + right.shape[1]] = dot(left, right, 0, 0).astype(BF16)
        start += right.shape[1]


def weight_grads(left_a, right_a, left_b, right_b):
    tile = 256
    args, specs, cols = [], [], 0
    for left, right in ((left_a, right_a), (left_b, right_b)):
        flat = [half for hop in HOPS for half in left[hop]]
        rows, width = flat[0].shape
        args += flat + [right[hop] for hop in HOPS]
        specs += [pl.BlockSpec((rows, tile), lambda i: (0, i))] * len(flat)
        specs += [whole(right[hop]) for hop in HOPS]
        cols += right[0].shape[1]
    out = shaped((width, cols), BF16)

    def body(*refs):
        weight_body(len(HOPS), *refs)

    out_spec = pl.BlockSpec((tile, cols), lambda i: (i, 0))
    flops = 2 * rows * 2 * len(HOPS) * width * cols
    return call(body, args, [out], 2 * flops, (width // tile,), specs, [out_spec])[0]


def stack_chunks(chunks):
    return jnp.concatenate([chunks[hop] for hop in HOPS], axis=0)


def on_device(
    layer_input,
    cotangent,
    segment,
    live_mask,
    query_weight,
    key_weight,
    value_weight,
    out_weight,
    up_weight,
    down_weight,
    query_bias,
    value_bias,
    up_bias,
    out_bias,
    down_bias,
    attention_gain,
    attention_shift,
    output_gain,
    output_shift,
):
    layers = query_weight.shape[0]
    core, high, x = lax.axis_index("c"), lax.axis_index("zh"), lax.axis_index("x")
    ring = lax.axis_size("x")
    owners = 16
    rows_in = swap_core_z(layer_input)

    head_cols = query_weight.shape[2]
    qkv_cols = 3 * head_cols
    shard_rows = query_weight.shape[1]
    ffn_half = up_weight.shape[2]
    qkv_shards = jnp.concatenate([query_weight, key_weight, value_weight], axis=2)

    turned_out = jnp.swapaxes(out_weight, 1, 2)
    first = swap_core_z(jnp.concatenate([qkv_shards[0], turned_out[0]], axis=1))
    spread = jnp.broadcast_to(first, (owners,) + first.shape)
    first = lax.all_to_all(spread, OWNERS, 0, 0, tiled=True).reshape(-1, first.shape[1])

    def gather_mat(*shards):
        mat = lax.all_gather(jnp.concatenate(shards, axis=1), DP, axis=0, tiled=True)
        return swap_core_z(mat)

    attn_mats, ffn_mats = [], []
    for layer in range(layers):
        if layer:
            attn_mats.append(gather_mat(qkv_shards[layer], turned_out[layer]))
        else:
            attn_mats.append(first)
        ffn_mats.append(gather_mat(up_weight[layer], jnp.swapaxes(down_weight[layer], 0, 1)))
    qkv_mats = [mat[:, :qkv_cols] for mat in attn_mats]
    out_mats = [mat[:, qkv_cols:] for mat in attn_mats]
    up_mats = [mat[:, :ffn_half] for mat in ffn_mats]
    down_mats = [mat[:, ffn_half:] for mat in ffn_mats]

    biases = jnp.concatenate([query_bias, value_bias, up_bias], axis=1)
    biases = swap_core_z(biases)
    query_bias = biases[:, :head_cols]
    value_bias = biases[:, head_cols : 2 * head_cols]
    up_bias = biases[:, 2 * head_cols :]

    packed = (segment * 2 + live_mask).astype(F32)
    packed = jnp.where(core == high, packed, other_core(packed)).reshape(2, ring, -1)
    packed = jnp.where(core == 0, packed, packed[::-1])
    ordered = []
    for hop in HOPS:
        ordered.append(lax.dynamic_index_in_dim(packed, lax.rem(x + ring - hop, ring), 1, False))
    marks = jnp.stack(ordered).reshape(len(HOPS), -1)
    seg_chunks = jnp.floor(marks * 0.5)
    live = (marks - 2 * seg_chunks).reshape(-1)
    key_mark = jnp.where(live > 0.5, seg_chunks.reshape(-1), -1.0)
    row_marks = {hop: seg_chunks[index][:, None] for index, hop in enumerate(HOPS)}
    key_mark = key_mark[None, :]

    current = rows_in.astype(F32)
    saved = []
    for layer in range(layers):
        qkv_mat, out_mat = qkv_mats[layer], out_mats[layer]
        up_mat, down_mat = up_mats[layer], down_mats[layer]
        qkv_bias = jnp.concatenate(
            [query_bias[layer], jnp.zeros_like(query_bias[layer]), value_bias[layer]]
        )
        inputs = gather_pairs(current.astype(BF16))
        qkv = {hop: make_qkv(inputs[hop], qkv_mat, qkv_bias[None, :]) for hop in ARRIVAL}
        keys = stack_chunks({hop: qkv[hop][1] for hop in HOPS})
        values = stack_chunks({hop: qkv[hop][2] for hop in HOPS})
        attended, soft, parts = {}, {}, {}
        for hop in ORDER:
            attended[hop], soft[hop], *parts[hop] = attend(
                qkv[hop][0], keys, values, row_marks[hop], key_mark, out_mat
            )
        first_sum = current + scatter_pairs(parts) + out_bias[layer]
        mid_unit, mid_scale = normalized(first_sum)
        normed_mid = mid_unit * attention_gain[layer] + attention_shift[layer]
        mids = gather_pairs(normed_mid.astype(BF16))
        activated, slopes, parts = {}, {}, {}
        for hop in ARRIVAL:
            activated[hop], slopes[hop], *parts[hop] = ffn(
                mids[hop], up_mat, up_bias[layer][None, :], down_mat
            )
        second_sum = normed_mid + scatter_pairs(parts) + down_bias[layer]
        out_unit, out_scale = normalized(second_sum)
        current = out_unit * output_gain[layer] + output_shift[layer]
        saved.append(
            (inputs, qkv, keys, values, attended, soft, mid_unit, mid_scale, mids, slopes,
             activated, out_unit, out_scale)
        )
    layer_output = swap_core_z(current.astype(BF16)).astype(F32)

    grad_rows = swap_core_z(cotangent).astype(F32)
    def sum_owners(terms):
        sent = terms.reshape(owners, shard_rows, terms.shape[1])
        return jnp.sum(lax.all_to_all(sent, OWNERS, 0, 0, tiled=True).astype(F32), axis=0)

    def sum_home(terms, layer):
        if layer:
            return lax.psum_scatter(swap_core_z(terms), DP, scatter_dimension=0, tiled=True)
        return swap_core_z(sum_owners(terms).astype(BF16))

    attn_cols = qkv_cols + head_cols
    attn_grads, ffn_grads = [None] * layers, [None] * layers
    head_sums, row_sums = [None] * layers, [None] * layers
    tail = None
    for layer in reversed(range(layers)):
        (inputs, qkv, keys, values, attended, soft, mid_unit, mid_scale, mids, slopes,
         activated, out_unit, out_scale) = saved[layer]
        qkv_mat, out_mat = qkv_mats[layer], out_mats[layer]
        up_mat, down_mat = up_mats[layer], down_mats[layer]
        grad_second, out_gain_term, out_shift_term = norm_back(
            grad_rows, out_unit, out_scale, output_gain[layer]
        )
        branch_low = grad_second.astype(BF16)
        down_bias_term = jnp.sum(branch_low.astype(F32), axis=0)
        branch = gather_pairs(branch_low)
        grad_pre, parts, up_sums = {}, {}, []
        for hop in ARRIVAL:
            grad_pre[hop], up_sum, *parts[hop] = ffn_back(
                branch[hop], up_mat, down_mat, slopes[hop]
            )
            up_sums.append(up_sum[0])
        grad_mid = grad_second + scatter_pairs(parts)
        up_bias_term = sum(up_sums)
        terms = weight_grads(mids, grad_pre, branch, activated)
        ffn_grads[layer] = sum_home(terms, layer)

        grad_first, att_gain_term, att_shift_term = norm_back(
            grad_mid, mid_unit, mid_scale, attention_gain[layer]
        )
        attn_low = grad_first.astype(BF16)
        out_bias_term = jnp.sum(attn_low.astype(F32), axis=0)
        attn_chunks = gather_pairs(attn_low)
        grad_q = {}
        grad_k, grad_v = jnp.zeros(keys.shape, F32), jnp.zeros(keys.shape, F32)
        for hop in ARRIVAL:
            grad_q[hop], grad_k, grad_v = attend_back(
                attn_chunks[hop], out_mat, qkv[hop][0], keys, values, soft[hop], grad_k, grad_v
            )
        parts, grad_qkv, sums = {}, {}, []
        for hop in ORDER:
            grad_qkv[hop], qkv_sum, *parts[hop] = inputs_back(
                grad_q[hop], grad_k, grad_v, HOPS.index(hop), qkv_mat
            )
            sums.append(qkv_sum[0])
        grad_rows = grad_first + scatter_pairs(parts)
        terms = weight_grads(inputs, grad_qkv, attn_chunks, attended)
        bias_terms = sum(sums)
        head_sums[layer] = jnp.concatenate(
            [bias_terms[:head_cols], bias_terms[2 * head_cols :], up_bias_term]
        )
        row_sums[layer] = jnp.stack(
            [out_bias_term, down_bias_term, att_gain_term, att_shift_term, out_gain_term,
             out_shift_term]
        )
        if layer > 0:
            attn_grads[layer] = sum_home(terms, layer)
        else:
            tail = terms

    slices = jnp.stack(row_sums).reshape(layers * 6, 2, ring, -1)
    slices = jnp.transpose(slices, (1, 2, 0, 3))
    mine = lax.dynamic_index_in_dim(slices, core, 0, False)
    send = lax.dynamic_index_in_dim(slices, 1 - core, 0, False)
    both = mine + other_core(send)
    kept = None
    for hop in HOPS:
        part = lax.dynamic_index_in_dim(both, lax.rem(x + ring - hop, ring), 0, False)
        part = along_x(part, -hop) if hop else part
        kept = part if kept is None else kept + part
    small = jnp.concatenate([jnp.stack(head_sums).reshape(-1), kept.reshape(-1)])
    small_len = small.shape[0]
    extra = -(-small_len // (16 * attn_cols)) * 16
    small_rows = jnp.pad(small, (0, extra * attn_cols - small_len)).reshape(1, extra, attn_cols)
    sent = jnp.concatenate(
        [
            tail.reshape(owners, shard_rows, attn_cols),
            jnp.broadcast_to(small_rows.astype(BF16), (owners, extra, attn_cols)),
        ],
        axis=1,
    )
    got = lax.all_to_all(sent, OWNERS, 0, 0, tiled=True)
    got = jnp.sum(got.astype(F32), axis=0)
    attn_grads[0] = swap_core_z(got[:shard_rows].astype(BF16))
    small = got[shard_rows:].reshape(-1)[:small_len]
    head_len = layers * head_sums[0].shape[0]

    bias_all = swap_core_z(small[:head_len].reshape(layers, -1))
    input_grad = swap_core_z(grad_rows.astype(BF16)).astype(F32)

    piece = small[head_len:].reshape(layers * 6, -1)
    table = jnp.zeros((2, ring) + piece.shape, F32)
    for hop in HOPS:
        one = along_x(piece, hop) if hop else piece
        where = lax.rem(x + ring - hop, ring)
        table = lax.dynamic_update_slice(table, one[None, None], (core, where, 0, 0))
    pair = lax.dynamic_slice_in_dim(table, core, 1, 0)
    table = lax.dynamic_update_slice(table, other_core(pair), (1 - core, 0, 0, 0))
    rows_out = jnp.transpose(table, (2, 0, 1, 3)).reshape(layers, 6, -1)

    def cols(pieces, start, count, turn=False):
        chosen = [piece[:, start : start + count].astype(F32) for piece in pieces]
        return jnp.stack([jnp.swapaxes(one, 0, 1) if turn else one for one in chosen])

    return (
        layer_output,
        input_grad,
        cols(attn_grads, 0, head_cols),
        cols(attn_grads, head_cols, head_cols),
        cols(attn_grads, 2 * head_cols, head_cols),
        cols(attn_grads, qkv_cols, head_cols, True),
        cols(ffn_grads, 0, ffn_half),
        cols(ffn_grads, ffn_half, ffn_half, True),
        bias_all[:, :head_cols],
        bias_all[:, head_cols : 2 * head_cols],
        bias_all[:, 2 * head_cols :],
        rows_out[:, 0],
        rows_out[:, 1],
        rows_out[:, 2],
        rows_out[:, 3],
        rows_out[:, 4],
        rows_out[:, 5],
    )


def solution(mesh):
    split = Mesh(mesh.devices.reshape(4, 2, 2, 2, 4), AXES)
    rows = P(DP + TENSOR, None)
    tall = P(None, DP, TENSOR)
    wide = P(None, TENSOR, DP)
    held = P(None, TENSOR)
    return jax.shard_map(
        on_device,
        mesh=split,
        in_specs=(rows, rows, P(DP), P(DP), tall, tall, tall, wide, tall, wide, held, held, held)
        + (P(),) * 6,
        out_specs=(rows, rows, tall, tall, tall, wide, tall, wide, held, held, held) + (P(),) * 6,
        check_vma=False,
    )
```

```python
import jax
import jax.numpy as jnp
from jax import lax
from jax.experimental import pallas as pl
from jax.experimental.pallas import tpu as pltpu
from jax.sharding import Mesh, PartitionSpec as P

HEAD_DIM = 64
NORM_EPS = 1e-12
MASKED = -1000000000.0
F32 = jnp.float32
BF16 = jnp.bfloat16

AXES = ("y", "zl", "c", "zh", "x")
DP = ("y", "zl", "c")
TENSOR = ("zh", "x")
OWNERS = ("y", "zl", "zh")
HOPS = (0, 1, 3, 2)
ORDER = (2, 1, 3, 0)
ARRIVAL = (0, 1, 3, 2)


def dot(left, right, left_dim, right_dim):
    return lax.dot_general(
        left, right, (((left_dim,), (right_dim,)), ((), ())), preferred_element_type=F32
    )


def along_x(value, hop):
    ring = lax.axis_size("x")
    return lax.ppermute(value, "x", [(i, (i + hop) % ring) for i in range(ring)])


def other_core(value):
    return lax.ppermute(value, "c", [(0, 1), (1, 0)])


def swap_core_z(value):
    ring = lax.axis_size("x")
    pairs = []
    for core in range(2):
        for high in range(2):
            for x in range(ring):
                pairs.append(((core * 2 + high) * ring + x, (high * 2 + core) * ring + x))
    return lax.ppermute(value, ("c", "zh", "x"), pairs)


def gather_pairs(rows):
    mine = {hop: along_x(rows, hop) if hop else rows for hop in (1, 3, 2, 0)}
    return {hop: (mine[hop], other_core(mine[hop])) for hop in ARRIVAL}


def scatter_pairs(parts):
    total = None
    for hop in ORDER:
        keep, send = parts[hop]
        both = keep + other_core(send).astype(F32)
        if hop:
            both = along_x(both.astype(BF16), -hop).astype(F32)
        total = both if total is None else total + both
    return total


def normalized(rows):
    center = rows - jnp.mean(rows, axis=-1, keepdims=True)
    spread = jnp.mean(center * center, axis=-1, keepdims=True)
    scale = lax.rsqrt(spread + NORM_EPS)
    return center * scale, scale


def norm_back(grad, unit, scale, gain):
    gain_grad = jnp.sum(grad * unit, axis=0)
    shift_grad = jnp.sum(grad, axis=0)
    scaled = grad * gain
    mean_all = jnp.mean(scaled, axis=-1, keepdims=True)
    mean_unit = jnp.mean(scaled * unit, axis=-1, keepdims=True)
    return scale * (scaled - mean_all - unit * mean_unit), gain_grad, shift_grad


def whole(array):
    rank = len(array.shape)
    return pl.BlockSpec(array.shape, lambda *_: (0,) * rank)


def call(body, args, outs, flops, grid=(), in_specs=None, out_specs=None, room=40):
    size = sum(a.size * a.dtype.itemsize for a in (*args, *outs))
    return pl.pallas_call(
        body,
        grid=grid,
        in_specs=in_specs or [whole(a) for a in args],
        out_specs=out_specs or [whole(o) for o in outs],
        out_shape=list(outs),
        compiler_params=pltpu.CompilerParams(vmem_limit_bytes=room * 1024 * 1024),
        cost_estimate=pl.CostEstimate(flops=flops, bytes_accessed=size, transcendentals=0),
    )(*args)


def shaped(shape, dtype):
    return jax.ShapeDtypeStruct(shape, dtype)


def both_rows(mine, other):
    return jnp.concatenate([mine[...], other[...]], axis=0)


def store_part(part, keep, send):
    half = keep.shape[0]
    keep[...] = part[:half]
    send[...] = part[half:].astype(BF16)


def part_shapes(rows, width):
    return [shaped((rows, width), F32), shaped((rows, width), BF16)]


def qkv_body(mine, other, mat, bias, query, key, value):
    out = (dot(both_rows(mine, other), mat[...], 1, 0) + bias[...]).astype(BF16)
    step = query.shape[1]
    query[...] = out[:, :step]
    key[...] = out[:, step : 2 * step]
    value[...] = out[:, 2 * step :]


def make_qkv(pair, mat, bias):
    rows, width = pair[0].shape
    out = shaped((2 * rows, mat.shape[1] // 3), BF16)
    return call(qkv_body, (*pair, mat, bias), [out] * 3, 4 * rows * mat.size)


def lanes_of(shape, head):
    return lax.broadcasted_iota(jnp.int32, shape, 1) // HEAD_DIM == head


def attend_body(query, key, value, row_mark, key_mark, out_mat, mixed, soft, keep, send):
    allowed = row_mark[...] == key_mark[...]
    total = jnp.zeros(query.shape, F32)
    for head in range(soft.shape[0]):
        lanes = lanes_of(query.shape, head)
        chosen = jnp.where(lanes, query[...], jnp.zeros(query.shape, BF16))
        scores = dot(chosen, key[...], 1, 1) * HEAD_DIM**-0.5
        scores = jnp.where(allowed, scores, MASKED)
        exps = jnp.exp(scores - jnp.max(scores, axis=-1, keepdims=True))
        probs = (exps * (1.0 / jnp.sum(exps, axis=-1, keepdims=True))).astype(BF16)
        soft[head] = probs
        total = jnp.where(lanes, dot(probs, value[...], 1, 0), total)
    low = total.astype(BF16)
    mixed[...] = low
    store_part(dot(low, out_mat[...], 1, 1), keep, send)


def attend(query, key, value, row_mark, key_mark, out_mat):
    rows, width = query.shape
    heads = width // HEAD_DIM
    outs = [shaped((rows, width), BF16), shaped((heads, rows, key.shape[0]), BF16)]
    outs += part_shapes(rows // 2, out_mat.shape[0])
    flops = 4 * heads * rows * key.size + 2 * rows * out_mat.size
    return call(attend_body, (query, key, value, row_mark, key_mark, out_mat), outs, 3 * flops)


def attend_back_body(mine, other, out_mat, query, key, value, soft, key_in, value_in, grad_query, key_out, value_out):
    grads = dot(both_rows(mine, other), out_mat[...], 1, 0).astype(BF16)
    for_query = jnp.zeros(query.shape, F32)
    for_key = jnp.zeros(key.shape, F32)
    for_value = jnp.zeros(key.shape, F32)
    for head in range(soft.shape[0]):
        lanes = lanes_of(query.shape, head)
        tall = lanes_of(key.shape, head)
        probs = soft[head]
        wide = probs.astype(F32)
        chosen = jnp.where(lanes, grads, jnp.zeros(query.shape, BF16))
        grad_soft = dot(chosen, value[...], 1, 1)
        row = jnp.sum(grad_soft * wide, axis=-1, keepdims=True)
        scores = (wide * (grad_soft - row)).astype(BF16)
        for_query = jnp.where(lanes, dot(scores, key[...], 1, 0), for_query)
        for_key = jnp.where(tall, dot(scores, query[...], 0, 0), for_key)
        for_value = jnp.where(tall, dot(probs, grads, 0, 0), for_value)
    grad_query[...] = (for_query * HEAD_DIM**-0.5).astype(BF16)
    key_out[...] = key_in[...] + for_key * HEAD_DIM**-0.5
    value_out[...] = value_in[...] + for_value


def attend_back(pair, out_mat, query, key, value, soft, key_sum, value_sum):
    outs = [shaped(query.shape, BF16), shaped(key.shape, F32), shaped(key.shape, F32)]
    args = (*pair, out_mat, query, key, value, soft, key_sum, value_sum)
    flops = 8 * soft.shape[0] * query.shape[0] * key.size
    return call(attend_back_body, args, outs, 2 * flops)


def inputs_back_body(grad_query, grad_key, grad_value, mat, joined, sums, keep, send):
    rows = jnp.concatenate(
        [grad_query[...], grad_key[...].astype(BF16), grad_value[...].astype(BF16)], axis=1
    )
    joined[...] = rows
    sums[...] = jnp.sum(rows.astype(F32), axis=0, keepdims=True)
    store_part(dot(rows, mat[...], 1, 1), keep, send)


def inputs_back(grad_query, grad_key, grad_value, index, mat):
    rows, width = grad_query.shape
    outs = [shaped((rows, 3 * width), BF16), shaped((1, 3 * width), F32)]
    outs += part_shapes(rows // 2, mat.shape[0])
    block = pl.BlockSpec((rows, width), lambda *_: (index, 0))
    args = (grad_query, grad_key, grad_value, mat)
    specs = [whole(grad_query), block, block, whole(mat)]
    return call(inputs_back_body, args, outs, 2 * rows * mat.size, (1,), specs)


def ffn_body(mine, other, up, bias, down, act, slope, keep, send):
    pre = dot(both_rows(mine, other), up[...], 1, 0) + bias[...]
    area = 0.5 + 0.5 * lax.erf(pre * 0.7071067811865476)
    low = (pre * area).astype(BF16)
    act[...] = low
    slope[...] = (area + pre * (jnp.exp(pre * pre * -0.5) * 0.3989422804014327)).astype(BF16)
    store_part(dot(low, down[...], 1, 1), keep, send)


def ffn(pair, up, bias, down):
    rows, width = pair[0].shape
    outs = [shaped((2 * rows, up.shape[1]), BF16)] * 2 + part_shapes(rows, width)
    return call(ffn_body, (*pair, up, bias, down), outs, 4 * rows * (up.size + down.size))


def ffn_back_body(mine, other, up, down, slope, grad, sums, keep, send):
    low = (dot(both_rows(mine, other), down[...], 1, 0) * slope[...].astype(F32)).astype(BF16)
    grad[...] = low
    sums[...] = jnp.sum(low.astype(F32), axis=0, keepdims=True)
    store_part(dot(low, up[...], 1, 1), keep, send)


def ffn_back(pair, up, down, slope):
    rows, width = pair[0].shape
    outs = [shaped(slope.shape, BF16), shaped((1, slope.shape[1]), F32)] + part_shapes(rows, width)
    return call(ffn_back_body, (*pair, up, down, slope), outs, 4 * rows * (up.size + down.size))


def weight_grads(pairs, owners, extra=None):
    count = len(HOPS)
    tile = 256
    args, specs, cols = [], [], 0
    for left, right in pairs:
        flat = [half for hop in HOPS for half in left[hop]]
        rows, width = flat[0].shape
        args += flat + [right[hop] for hop in HOPS]
        specs += [pl.BlockSpec((rows, tile), lambda i: (0, i))] * len(flat)
        specs += [whole(right[hop]) for hop in HOPS]
        cols += right[0].shape[1]
    slab = width // owners
    depth = slab
    if extra is not None:
        args.append(extra)
        specs.append(whole(extra))
        depth += extra.shape[0]

    def body(*refs):
        out = refs[-1]
        start = 0
        for index in range(len(pairs)):
            here = refs[index * 3 * count : (index + 1) * 3 * count]
            left = jnp.concatenate([ref[...] for ref in here[: 2 * count]], axis=0)
            right = jnp.concatenate([ref[...] for ref in here[2 * count :]], axis=0)
            end = start + right.shape[1]
            found = dot(left, right, 0, 0).astype(BF16)
            for part in range(tile // slab):
                out[part, :slab, start:end] = found[part * slab : (part + 1) * slab]
            start = end
        if extra is not None:
            for part in range(tile // slab):
                out[part, slab:, :] = refs[-2][...]

    out = shaped((owners, depth, cols), BF16)
    out_spec = pl.BlockSpec((tile // slab, depth, cols), lambda i: (i, 0, 0))
    flops = 2 * rows * 2 * count * width * cols
    return call(body, args, [out], 2 * flops, (width // tile,), specs, [out_spec], 58)[0]


def stack_chunks(chunks):
    return jnp.concatenate([chunks[hop] for hop in HOPS], axis=0)


def sum_group(vectors, core, x):
    ring = lax.axis_size("x")
    slices = vectors.reshape(vectors.shape[0], 2, ring, -1)
    slices = jnp.transpose(slices, (1, 2, 0, 3))
    mine = lax.dynamic_index_in_dim(slices, core, 0, False)
    send = lax.dynamic_index_in_dim(slices, 1 - core, 0, False)
    both = mine + other_core(send)
    kept = None
    for hop in HOPS:
        part = lax.dynamic_index_in_dim(both, lax.rem(x + ring - hop, ring), 0, False)
        part = along_x(part, -hop) if hop else part
        kept = part if kept is None else kept + part
    return kept


def on_device(
    layer_input,
    cotangent,
    segment,
    live_mask,
    query_weight,
    key_weight,
    value_weight,
    out_weight,
    up_weight,
    down_weight,
    query_bias,
    value_bias,
    up_bias,
    out_bias,
    down_bias,
    attention_gain,
    attention_shift,
    output_gain,
    output_shift,
):
    layers = query_weight.shape[0]
    core, high, x = lax.axis_index("c"), lax.axis_index("zh"), lax.axis_index("x")
    ring = lax.axis_size("x")
    owners = 16
    rows_in = swap_core_z(layer_input)

    head_cols = query_weight.shape[2]
    qkv_cols = 3 * head_cols
    shard_rows = query_weight.shape[1]
    ffn_half = up_weight.shape[2]
    qkv_shards = jnp.concatenate([query_weight, key_weight, value_weight], axis=2)

    turned_out = jnp.swapaxes(out_weight, 1, 2)
    first = swap_core_z(jnp.concatenate([qkv_shards[0], turned_out[0]], axis=1))
    spread = jnp.broadcast_to(first, (owners,) + first.shape)
    first = lax.all_to_all(spread, OWNERS, 0, 0, tiled=True).reshape(-1, first.shape[1])

    def gather_mat(*shards):
        mat = lax.all_gather(jnp.concatenate(shards, axis=1), DP, axis=0, tiled=True)
        return swap_core_z(mat)

    attn_mats, ffn_mats = [], []
    for layer in range(layers):
        if layer:
            attn_mats.append(gather_mat(qkv_shards[layer], turned_out[layer]))
        else:
            attn_mats.append(first)
        ffn_mats.append(gather_mat(up_weight[layer], jnp.swapaxes(down_weight[layer], 0, 1)))
    qkv_mats = [mat[:, :qkv_cols] for mat in attn_mats]
    out_mats = [mat[:, qkv_cols:] for mat in attn_mats]
    up_mats = [mat[:, :ffn_half] for mat in ffn_mats]
    down_mats = [mat[:, ffn_half:] for mat in ffn_mats]

    biases = jnp.concatenate([query_bias, value_bias, up_bias], axis=1)
    biases = swap_core_z(biases)
    query_bias = biases[:, :head_cols]
    value_bias = biases[:, head_cols : 2 * head_cols]
    up_bias = biases[:, 2 * head_cols :]

    packed = (segment * 2 + live_mask).astype(F32)
    packed = jnp.where(core == high, packed, other_core(packed)).reshape(2, ring, -1)
    packed = jnp.where(core == 0, packed, packed[::-1])
    ordered = []
    for hop in HOPS:
        ordered.append(lax.dynamic_index_in_dim(packed, lax.rem(x + ring - hop, ring), 1, False))
    marks = jnp.stack(ordered).reshape(len(HOPS), -1)
    seg_chunks = jnp.floor(marks * 0.5)
    live = (marks - 2 * seg_chunks).reshape(-1)
    key_mark = jnp.where(live > 0.5, seg_chunks.reshape(-1), -1.0)
    row_marks = {hop: seg_chunks[index][:, None] for index, hop in enumerate(HOPS)}
    key_mark = key_mark[None, :]

    current = rows_in.astype(F32)
    saved = []
    for layer in range(layers):
        qkv_mat, out_mat = qkv_mats[layer], out_mats[layer]
        up_mat, down_mat = up_mats[layer], down_mats[layer]
        qkv_bias = jnp.concatenate(
            [query_bias[layer], jnp.zeros_like(query_bias[layer]), value_bias[layer]]
        )
        inputs = gather_pairs(current.astype(BF16))
        qkv = {hop: make_qkv(inputs[hop], qkv_mat, qkv_bias[None, :]) for hop in ARRIVAL}
        keys = stack_chunks({hop: qkv[hop][1] for hop in HOPS})
        values = stack_chunks({hop: qkv[hop][2] for hop in HOPS})
        attended, soft, parts = {}, {}, {}
        for hop in ORDER:
            attended[hop], soft[hop], *parts[hop] = attend(
                qkv[hop][0], keys, values, row_marks[hop], key_mark, out_mat
            )
        first_sum = current + scatter_pairs(parts) + out_bias[layer]
        mid_unit, mid_scale = normalized(first_sum)
        normed_mid = mid_unit * attention_gain[layer] + attention_shift[layer]
        mids = gather_pairs(normed_mid.astype(BF16))
        activated, slopes, parts = {}, {}, {}
        for hop in ARRIVAL:
            activated[hop], slopes[hop], *parts[hop] = ffn(
                mids[hop], up_mat, up_bias[layer][None, :], down_mat
            )
        second_sum = normed_mid + scatter_pairs(parts) + down_bias[layer]
        out_unit, out_scale = normalized(second_sum)
        current = out_unit * output_gain[layer] + output_shift[layer]
        saved.append(
            (inputs, qkv, keys, values, attended, soft, mid_unit, mid_scale, mids, slopes,
             activated, out_unit, out_scale)
        )
    layer_output = swap_core_z(current.astype(BF16)).astype(F32)

    grad_rows = swap_core_z(cotangent).astype(F32)
    def sum_owners(terms):
        return jnp.sum(lax.all_to_all(terms, OWNERS, 0, 0, tiled=True).astype(F32), axis=0)

    def extra_rows(values, cols):
        count = -(-values.shape[0] // (16 * cols)) * 16
        padded = jnp.pad(values, (0, count * cols - values.shape[0]))
        return padded.reshape(count, cols).astype(BF16)

    late_grads, qkv_grads = [None] * layers, [None] * layers
    row_sums, head_sums, waiting = [], [], []
    for layer in reversed(range(layers)):
        (inputs, qkv, keys, values, attended, soft, mid_unit, mid_scale, mids, slopes,
         activated, out_unit, out_scale) = saved[layer]
        qkv_mat, out_mat = qkv_mats[layer], out_mats[layer]
        up_mat, down_mat = up_mats[layer], down_mats[layer]
        grad_second, out_gain_term, out_shift_term = norm_back(
            grad_rows, out_unit, out_scale, output_gain[layer]
        )
        branch_low = grad_second.astype(BF16)
        down_bias_term = jnp.sum(branch_low.astype(F32), axis=0)
        branch = gather_pairs(branch_low)
        grad_pre, parts, up_sums = {}, {}, []
        for hop in ARRIVAL:
            grad_pre[hop], up_sum, *parts[hop] = ffn_back(
                branch[hop], up_mat, down_mat, slopes[hop]
            )
            up_sums.append(up_sum[0])
        grad_mid = grad_second + scatter_pairs(parts)
        up_bias_term = sum(up_sums)
        grad_first, att_gain_term, att_shift_term = norm_back(
            grad_mid, mid_unit, mid_scale, attention_gain[layer]
        )
        attn_low = grad_first.astype(BF16)
        out_bias_term = jnp.sum(attn_low.astype(F32), axis=0)
        attn_chunks = gather_pairs(attn_low)
        row_sums.append(
            jnp.stack([out_bias_term, down_bias_term, att_gain_term, att_shift_term, out_gain_term,
                       out_shift_term])
        )
        head_sums.append(up_bias_term)
        late = [(mids, grad_pre), (branch, activated), (attn_chunks, attended)]
        if layer:
            terms = weight_grads(late, owners)
            found = lax.psum_scatter(terms, OWNERS, scatter_dimension=0, tiled=False)
            late_grads[layer] = swap_core_z(found)
        else:
            kept = sum_group(jnp.concatenate(row_sums), core, x)
            small = jnp.concatenate(head_sums + [kept.reshape(-1)])
            cols = sum(right[0].shape[1] for _, right in late + waiting)
            terms = weight_grads(late + waiting, owners, extra_rows(small, cols))
            joint = sum_owners(terms)
            early_sums = joint[shard_rows:].reshape(-1)[: small.shape[0]]
            joint = swap_core_z(joint[:shard_rows].astype(BF16))
            late_cols = cols - (layers - 1) * qkv_cols
            late_grads[0] = joint[:, :late_cols]
            for index in range(1, layers):
                start = late_cols + (layers - 1 - index) * qkv_cols
                qkv_grads[index] = joint[:, start : start + qkv_cols]
        grad_q = {}
        grad_k, grad_v = jnp.zeros(keys.shape, F32), jnp.zeros(keys.shape, F32)
        for hop in ARRIVAL:
            grad_q[hop], grad_k, grad_v = attend_back(
                attn_chunks[hop], out_mat, qkv[hop][0], keys, values, soft[hop], grad_k, grad_v
            )
        parts, grad_qkv, sums = {}, {}, []
        for hop in ORDER:
            grad_qkv[hop], qkv_sum, *parts[hop] = inputs_back(
                grad_q[hop], grad_k, grad_v, HOPS.index(hop), qkv_mat
            )
            sums.append(qkv_sum[0])
        grad_rows = grad_first + scatter_pairs(parts)
        bias_terms = sum(sums)
        pair_sums = jnp.concatenate([bias_terms[:head_cols], bias_terms[2 * head_cols :]])
        if layer:
            waiting.append((inputs, grad_qkv))
            head_sums.append(pair_sums)
        else:
            terms = weight_grads([(inputs, grad_qkv)], owners, extra_rows(pair_sums, qkv_cols))
            got = sum_owners(terms)
            qkv_grads[0] = swap_core_z(got[:shard_rows].astype(BF16))
            last_sums = got[shard_rows:].reshape(-1)[: 2 * head_cols]

    head_len = sum(item.shape[0] for item in head_sums)
    ups, pairs, place = [None] * layers, [last_sums] + [None] * (layers - 1), 0
    for layer in reversed(range(layers)):
        ups[layer] = early_sums[place : place + ffn_half]
        place += ffn_half
        if layer:
            pairs[layer] = early_sums[place : place + 2 * head_cols]
            place += 2 * head_cols
    up_all = swap_core_z(jnp.stack(ups))
    pair_all = swap_core_z(jnp.stack(pairs))
    input_grad = swap_core_z(grad_rows.astype(BF16)).astype(F32)

    piece = early_sums[head_len:].reshape(layers * 6, -1)
    table = jnp.zeros((2, ring) + piece.shape, F32)
    for hop in HOPS:
        one = along_x(piece, hop) if hop else piece
        where = lax.rem(x + ring - hop, ring)
        table = lax.dynamic_update_slice(table, one[None, None], (core, where, 0, 0))
    pair = lax.dynamic_slice_in_dim(table, core, 1, 0)
    table = lax.dynamic_update_slice(table, other_core(pair), (1 - core, 0, 0, 0))
    rows_out = jnp.transpose(table, (2, 0, 1, 3)).reshape(layers, 6, -1)[::-1]

    def cols(pieces, start, count, turn=False):
        chosen = [piece[:, start : start + count].astype(F32) for piece in pieces]
        return jnp.stack([jnp.swapaxes(one, 0, 1) if turn else one for one in chosen])

    return (
        layer_output,
        input_grad,
        cols(qkv_grads, 0, head_cols),
        cols(qkv_grads, head_cols, head_cols),
        cols(qkv_grads, 2 * head_cols, head_cols),
        cols(late_grads, 2 * ffn_half, head_cols, True),
        cols(late_grads, 0, ffn_half),
        cols(late_grads, ffn_half, ffn_half, True),
        pair_all[:, :head_cols],
        pair_all[:, head_cols:],
        up_all,
        rows_out[:, 0],
        rows_out[:, 1],
        rows_out[:, 2],
        rows_out[:, 3],
        rows_out[:, 4],
        rows_out[:, 5],
    )


def solution(mesh):
    split = Mesh(mesh.devices.reshape(4, 2, 2, 2, 4), AXES)
    rows = P(DP + TENSOR, None)
    tall = P(None, DP, TENSOR)
    wide = P(None, TENSOR, DP)
    held = P(None, TENSOR)
    return jax.shard_map(
        on_device,
        mesh=split,
        in_specs=(rows, rows, P(DP), P(DP), tall, tall, tall, wide, tall, wide, held, held, held)
        + (P(),) * 6,
        out_specs=(rows, rows, tall, tall, tall, wide, tall, wide, held, held, held) + (P(),) * 6,
        check_vma=False,
    )
```

```python
import jax
import jax.numpy as jnp
from jax import lax
from jax.experimental import pallas as pl
from jax.experimental.pallas import tpu as pltpu
from jax.sharding import Mesh, PartitionSpec as P

HEAD_DIM = 64
NORM_EPS = 1e-12
MASKED = -1000000000.0
F32 = jnp.float32
BF16 = jnp.bfloat16

AXES = ("y", "zl", "c", "zh", "x")
DP = ("y", "zl", "c")
TENSOR = ("zh", "x")
OWNERS = ("y", "zl", "zh")
HOPS = (0, 1, 3, 2)
ORDER = (2, 1, 3, 0)
ARRIVAL = (0, 1, 3, 2)


def dot(left, right, left_dim, right_dim):
    return lax.dot_general(
        left, right, (((left_dim,), (right_dim,)), ((), ())), preferred_element_type=F32
    )


def along_x(value, hop):
    ring = lax.axis_size("x")
    return lax.ppermute(value, "x", [(i, (i + hop) % ring) for i in range(ring)])


def other_core(value):
    return lax.ppermute(value, "c", [(0, 1), (1, 0)])


def swap_core_z(value):
    ring = lax.axis_size("x")
    pairs = []
    for core in range(2):
        for high in range(2):
            for x in range(ring):
                pairs.append(((core * 2 + high) * ring + x, (high * 2 + core) * ring + x))
    return lax.ppermute(value, ("c", "zh", "x"), pairs)


def gather_pairs(rows):
    mine = {hop: along_x(rows, hop) if hop else rows for hop in (1, 3, 2, 0)}
    return {hop: (mine[hop], other_core(mine[hop])) for hop in ARRIVAL}


def scatter_pairs(parts):
    total = None
    for hop in ORDER:
        keep, send = parts[hop]
        both = keep + other_core(send).astype(F32)
        if hop:
            both = along_x(both.astype(BF16), -hop).astype(F32)
        total = both if total is None else total + both
    return total


def normalized(rows):
    center = rows - jnp.mean(rows, axis=-1, keepdims=True)
    spread = jnp.mean(center * center, axis=-1, keepdims=True)
    scale = lax.rsqrt(spread + NORM_EPS)
    return center * scale, scale


def norm_back(grad, unit, scale, gain):
    gain_grad = jnp.sum(grad * unit, axis=0)
    shift_grad = jnp.sum(grad, axis=0)
    scaled = grad * gain
    mean_all = jnp.mean(scaled, axis=-1, keepdims=True)
    mean_unit = jnp.mean(scaled * unit, axis=-1, keepdims=True)
    return scale * (scaled - mean_all - unit * mean_unit), gain_grad, shift_grad


def whole(array):
    rank = len(array.shape)
    return pl.BlockSpec(array.shape, lambda *_: (0,) * rank)


def call(body, args, outs, flops, grid=(), in_specs=None, out_specs=None, room=40):
    size = sum(a.size * a.dtype.itemsize for a in (*args, *outs))
    return pl.pallas_call(
        body,
        grid=grid,
        in_specs=in_specs or [whole(a) for a in args],
        out_specs=out_specs or [whole(o) for o in outs],
        out_shape=list(outs),
        compiler_params=pltpu.CompilerParams(vmem_limit_bytes=room * 1024 * 1024),
        cost_estimate=pl.CostEstimate(flops=flops, bytes_accessed=size, transcendentals=0),
    )(*args)


def shaped(shape, dtype):
    return jax.ShapeDtypeStruct(shape, dtype)


def both_rows(mine, other):
    return jnp.concatenate([mine[...], other[...]], axis=0)


def store_part(part, keep, send):
    half = keep.shape[0]
    keep[...] = part[:half]
    send[...] = part[half:].astype(BF16)


def part_shapes(rows, width):
    return [shaped((rows, width), F32), shaped((rows, width), BF16)]


def qkv_body(mine, other, mat, bias, query, key, value):
    out = (dot(both_rows(mine, other), mat[...], 1, 0) + bias[...]).astype(BF16)
    step = query.shape[1]
    query[...] = out[:, :step]
    key[...] = out[:, step : 2 * step]
    value[...] = out[:, 2 * step :]


def make_qkv(pair, mat, bias):
    rows, width = pair[0].shape
    out = shaped((2 * rows, mat.shape[1] // 3), BF16)
    return call(qkv_body, (*pair, mat, bias), [out] * 3, 4 * rows * mat.size)


def lanes_of(shape, head):
    return lax.broadcasted_iota(jnp.int32, shape, 1) // HEAD_DIM == head


def attend_body(query, key, value, row_mark, key_mark, out_mat, mixed, soft, keep, send):
    allowed = row_mark[...] == key_mark[...]
    total = jnp.zeros(query.shape, F32)
    for head in range(soft.shape[0]):
        lanes = lanes_of(query.shape, head)
        chosen = jnp.where(lanes, query[...], jnp.zeros(query.shape, BF16))
        scores = dot(chosen, key[...], 1, 1) * HEAD_DIM**-0.5
        scores = jnp.where(allowed, scores, MASKED)
        exps = jnp.exp(scores - jnp.max(scores, axis=-1, keepdims=True))
        probs = (exps * (1.0 / jnp.sum(exps, axis=-1, keepdims=True))).astype(BF16)
        soft[head] = probs
        total = jnp.where(lanes, dot(probs, value[...], 1, 0), total)
    low = total.astype(BF16)
    mixed[...] = low
    store_part(dot(low, out_mat[...], 1, 1), keep, send)


def attend(query, key, value, row_mark, key_mark, out_mat):
    rows, width = query.shape
    heads = width // HEAD_DIM
    outs = [shaped((rows, width), BF16), shaped((heads, rows, key.shape[0]), BF16)]
    outs += part_shapes(rows // 2, out_mat.shape[0])
    flops = 4 * heads * rows * key.size + 2 * rows * out_mat.size
    return call(attend_body, (query, key, value, row_mark, key_mark, out_mat), outs, 3 * flops)


def attend_back_body(mine, other, out_mat, query, key, value, soft, key_in, value_in, grad_query, key_out, value_out):
    grads = dot(both_rows(mine, other), out_mat[...], 1, 0).astype(BF16)
    for_query = jnp.zeros(query.shape, F32)
    for_key = jnp.zeros(key.shape, F32)
    for_value = jnp.zeros(key.shape, F32)
    for head in range(soft.shape[0]):
        lanes = lanes_of(query.shape, head)
        tall = lanes_of(key.shape, head)
        probs = soft[head]
        wide = probs.astype(F32)
        chosen = jnp.where(lanes, grads, jnp.zeros(query.shape, BF16))
        grad_soft = dot(chosen, value[...], 1, 1)
        row = jnp.sum(grad_soft * wide, axis=-1, keepdims=True)
        scores = (wide * (grad_soft - row)).astype(BF16)
        for_query = jnp.where(lanes, dot(scores, key[...], 1, 0), for_query)
        for_key = jnp.where(tall, dot(scores, query[...], 0, 0), for_key)
        for_value = jnp.where(tall, dot(probs, grads, 0, 0), for_value)
    grad_query[...] = (for_query * HEAD_DIM**-0.5).astype(BF16)
    key_out[...] = key_in[...] + for_key * HEAD_DIM**-0.5
    value_out[...] = value_in[...] + for_value


def attend_back(pair, out_mat, query, key, value, soft, key_sum, value_sum):
    outs = [shaped(query.shape, BF16), shaped(key.shape, F32), shaped(key.shape, F32)]
    args = (*pair, out_mat, query, key, value, soft, key_sum, value_sum)
    flops = 8 * soft.shape[0] * query.shape[0] * key.size
    return call(attend_back_body, args, outs, 2 * flops)


def inputs_back_body(grad_query, grad_key, grad_value, mat, joined, sums, keep, send):
    rows = jnp.concatenate(
        [grad_query[...], grad_key[...].astype(BF16), grad_value[...].astype(BF16)], axis=1
    )
    joined[...] = rows
    sums[...] = jnp.sum(rows.astype(F32), axis=0, keepdims=True)
    store_part(dot(rows, mat[...], 1, 1), keep, send)


def inputs_back(grad_query, grad_key, grad_value, index, mat):
    rows, width = grad_query.shape
    outs = [shaped((rows, 3 * width), BF16), shaped((1, 3 * width), F32)]
    outs += part_shapes(rows // 2, mat.shape[0])
    block = pl.BlockSpec((rows, width), lambda *_: (index, 0))
    args = (grad_query, grad_key, grad_value, mat)
    specs = [whole(grad_query), block, block, whole(mat)]
    return call(inputs_back_body, args, outs, 2 * rows * mat.size, (1,), specs)


def ffn_body(mine, other, up, bias, down, act, slope, keep, send):
    pre = dot(both_rows(mine, other), up[...], 1, 0) + bias[...]
    area = 0.5 + 0.5 * lax.erf(pre * 0.7071067811865476)
    low = (pre * area).astype(BF16)
    act[...] = low
    slope[...] = (area + pre * (jnp.exp(pre * pre * -0.5) * 0.3989422804014327)).astype(BF16)
    store_part(dot(low, down[...], 1, 1), keep, send)


def ffn(pair, up, bias, down):
    rows, width = pair[0].shape
    outs = [shaped((2 * rows, up.shape[1]), BF16)] * 2 + part_shapes(rows, width)
    return call(ffn_body, (*pair, up, bias, down), outs, 4 * rows * (up.size + down.size))


def ffn_back_body(mine, other, up, down, slope, grad, sums, keep, send):
    low = (dot(both_rows(mine, other), down[...], 1, 0) * slope[...].astype(F32)).astype(BF16)
    grad[...] = low
    sums[...] = jnp.sum(low.astype(F32), axis=0, keepdims=True)
    store_part(dot(low, up[...], 1, 1), keep, send)


def ffn_back(pair, up, down, slope):
    rows, width = pair[0].shape
    outs = [shaped(slope.shape, BF16), shaped((1, slope.shape[1]), F32)] + part_shapes(rows, width)
    return call(ffn_back_body, (*pair, up, down, slope), outs, 4 * rows * (up.size + down.size))


def weight_grads(pairs, owners, extra=None):
    count = len(HOPS)
    tile = 256
    args, specs, cols = [], [], 0
    for left, right in pairs:
        flat = [half for hop in HOPS for half in left[hop]]
        rows, width = flat[0].shape
        args += flat + [right[hop] for hop in HOPS]
        specs += [pl.BlockSpec((rows, tile), lambda i: (0, i))] * len(flat)
        specs += [whole(right[hop]) for hop in HOPS]
        cols += right[0].shape[1]
    slab = width // owners
    depth = slab
    if extra is not None:
        args.append(extra)
        specs.append(whole(extra))
        depth += extra.shape[0]

    def body(*refs):
        out = refs[-1]
        start = 0
        for index in range(len(pairs)):
            here = refs[index * 3 * count : (index + 1) * 3 * count]
            left = jnp.concatenate([ref[...] for ref in here[: 2 * count]], axis=0)
            right = jnp.concatenate([ref[...] for ref in here[2 * count :]], axis=0)
            end = start + right.shape[1]
            found = dot(left, right, 0, 0).astype(BF16)
            for part in range(tile // slab):
                out[part, :slab, start:end] = found[part * slab : (part + 1) * slab]
            start = end
        if extra is not None:
            for part in range(tile // slab):
                out[part, slab:, :] = refs[-2][...]

    out = shaped((owners, depth, cols), BF16)
    out_spec = pl.BlockSpec((tile // slab, depth, cols), lambda i: (i, 0, 0))
    flops = 2 * rows * 2 * count * width * cols
    return call(body, args, [out], 2 * flops, (width // tile,), specs, [out_spec], 58)[0]


def stack_chunks(chunks):
    return jnp.concatenate([chunks[hop] for hop in HOPS], axis=0)


def sum_group(vectors, core, x):
    ring = lax.axis_size("x")
    slices = vectors.reshape(vectors.shape[0], 2, ring, -1)
    slices = jnp.transpose(slices, (1, 2, 0, 3))
    mine = lax.dynamic_index_in_dim(slices, core, 0, False)
    send = lax.dynamic_index_in_dim(slices, 1 - core, 0, False)
    both = mine + other_core(send)
    kept = None
    for hop in HOPS:
        part = lax.dynamic_index_in_dim(both, lax.rem(x + ring - hop, ring), 0, False)
        part = along_x(part, -hop) if hop else part
        kept = part if kept is None else kept + part
    return kept


def on_device(
    layer_input,
    cotangent,
    segment,
    live_mask,
    query_weight,
    key_weight,
    value_weight,
    out_weight,
    up_weight,
    down_weight,
    query_bias,
    value_bias,
    up_bias,
    out_bias,
    down_bias,
    attention_gain,
    attention_shift,
    output_gain,
    output_shift,
):
    layers = query_weight.shape[0]
    core, high, x = lax.axis_index("c"), lax.axis_index("zh"), lax.axis_index("x")
    ring = lax.axis_size("x")
    owners = 16
    rows_in = swap_core_z(layer_input)

    head_cols = query_weight.shape[2]
    qkv_cols = 3 * head_cols
    shard_rows = query_weight.shape[1]
    ffn_half = up_weight.shape[2]
    qkv_shards = jnp.concatenate([query_weight, key_weight, value_weight], axis=2)

    turned_out = jnp.swapaxes(out_weight, 1, 2)
    first = swap_core_z(jnp.concatenate([qkv_shards[0], turned_out[0]], axis=1))
    spread = jnp.broadcast_to(first, (owners,) + first.shape)
    first = lax.all_to_all(spread, OWNERS, 0, 0, tiled=True).reshape(-1, first.shape[1])

    def gather_mat(*shards):
        mat = lax.all_gather(jnp.concatenate(shards, axis=1), DP, axis=0, tiled=True)
        return swap_core_z(mat)

    attn_mats, ffn_mats = [], []
    for layer in range(layers):
        if layer:
            attn_mats.append(gather_mat(qkv_shards[layer], turned_out[layer]))
        else:
            attn_mats.append(first)
        ffn_mats.append(gather_mat(up_weight[layer], jnp.swapaxes(down_weight[layer], 0, 1)))
    qkv_mats = [mat[:, :qkv_cols] for mat in attn_mats]
    out_mats = [mat[:, qkv_cols:] for mat in attn_mats]
    up_mats = [mat[:, :ffn_half] for mat in ffn_mats]
    down_mats = [mat[:, ffn_half:] for mat in ffn_mats]

    biases = jnp.concatenate([query_bias, value_bias, up_bias], axis=1)
    biases = swap_core_z(biases)
    query_bias = biases[:, :head_cols]
    value_bias = biases[:, head_cols : 2 * head_cols]
    up_bias = biases[:, 2 * head_cols :]

    packed = (segment * 2 + live_mask).astype(F32)
    packed = jnp.where(core == high, packed, other_core(packed)).reshape(2, ring, -1)
    packed = jnp.where(core == 0, packed, packed[::-1])
    ordered = []
    for hop in HOPS:
        ordered.append(lax.dynamic_index_in_dim(packed, lax.rem(x + ring - hop, ring), 1, False))
    marks = jnp.stack(ordered).reshape(len(HOPS), -1)
    seg_chunks = jnp.floor(marks * 0.5)
    live = (marks - 2 * seg_chunks).reshape(-1)
    key_mark = jnp.where(live > 0.5, seg_chunks.reshape(-1), -1.0)
    row_marks = {hop: seg_chunks[index][:, None] for index, hop in enumerate(HOPS)}
    key_mark = key_mark[None, :]

    current = rows_in.astype(F32)
    saved = []
    for layer in range(layers):
        qkv_mat, out_mat = qkv_mats[layer], out_mats[layer]
        up_mat, down_mat = up_mats[layer], down_mats[layer]
        qkv_bias = jnp.concatenate(
            [query_bias[layer], jnp.zeros_like(query_bias[layer]), value_bias[layer]]
        )
        inputs = gather_pairs(current.astype(BF16))
        qkv = {hop: make_qkv(inputs[hop], qkv_mat, qkv_bias[None, :]) for hop in ARRIVAL}
        keys = stack_chunks({hop: qkv[hop][1] for hop in HOPS})
        values = stack_chunks({hop: qkv[hop][2] for hop in HOPS})
        attended, soft, parts = {}, {}, {}
        for hop in ORDER:
            attended[hop], soft[hop], *parts[hop] = attend(
                qkv[hop][0], keys, values, row_marks[hop], key_mark, out_mat
            )
        first_sum = current + scatter_pairs(parts) + out_bias[layer]
        mid_unit, mid_scale = normalized(first_sum)
        normed_mid = mid_unit * attention_gain[layer] + attention_shift[layer]
        mids = gather_pairs(normed_mid.astype(BF16))
        activated, slopes, parts = {}, {}, {}
        for hop in ARRIVAL:
            activated[hop], slopes[hop], *parts[hop] = ffn(
                mids[hop], up_mat, up_bias[layer][None, :], down_mat
            )
        second_sum = normed_mid + scatter_pairs(parts) + down_bias[layer]
        out_unit, out_scale = normalized(second_sum)
        current = out_unit * output_gain[layer] + output_shift[layer]
        saved.append(
            (inputs, qkv, keys, values, attended, soft, mid_unit, mid_scale, mids, slopes,
             activated, out_unit, out_scale)
        )
    layer_output = swap_core_z(current.astype(BF16)).astype(F32)

    grad_rows = swap_core_z(cotangent).astype(F32)
    attn_cols = qkv_cols + head_cols

    def sum_owners(terms):
        return jnp.sum(lax.all_to_all(terms, OWNERS, 0, 0, tiled=True).astype(F32), axis=0)

    def extra_rows(values, cols):
        count = -(-values.shape[0] // (16 * cols)) * 16
        padded = jnp.pad(values, (0, count * cols - values.shape[0]))
        return padded.reshape(count, cols).astype(BF16)

    ffn_grads, attn_grads = [None] * layers, [None] * layers
    row_sums, head_sums, pending = [], [], None
    tie = lax.optimization_barrier
    for layer in reversed(range(layers)):
        (inputs, qkv, keys, values, attended, soft, mid_unit, mid_scale, mids, slopes,
         activated, out_unit, out_scale) = saved[layer]
        qkv_mat, out_mat = qkv_mats[layer], out_mats[layer]
        up_mat, down_mat = up_mats[layer], down_mats[layer]
        grad_second, out_gain_term, out_shift_term = norm_back(
            grad_rows, out_unit, out_scale, output_gain[layer]
        )
        branch_low = grad_second.astype(BF16)
        down_bias_term = jnp.sum(branch_low.astype(F32), axis=0)
        branch = gather_pairs(branch_low)
        grad_pre, parts, up_sums = {}, {}, []
        for hop in ARRIVAL:
            grad_pre[hop], up_sum, *parts[hop] = ffn_back(
                branch[hop], up_mat, down_mat, slopes[hop]
            )
            up_sums.append(up_sum[0])
        grad_mid = grad_second + scatter_pairs(parts)
        up_bias_term = sum(up_sums)
        ffn_pairs = [(mids, grad_pre), (branch, activated)]
        if layer:
            grad_mid, terms = tie((grad_mid, weight_grads(ffn_pairs, owners)))
            found = sum_owners(terms)
        if pending is not None:
            grad_mid, pending = tie((grad_mid, pending))
            attn_grads[layer + 1] = swap_core_z(pending.astype(BF16))
        grad_first, att_gain_term, att_shift_term = norm_back(
            grad_mid, mid_unit, mid_scale, attention_gain[layer]
        )
        attn_low = grad_first.astype(BF16)
        out_bias_term = jnp.sum(attn_low.astype(F32), axis=0)
        attn_chunks = gather_pairs(attn_low)
        row_sums.append(
            jnp.stack([out_bias_term, down_bias_term, att_gain_term, att_shift_term, out_gain_term,
                       out_shift_term])
        )
        head_sums.append(up_bias_term)
        if not layer:
            kept = sum_group(jnp.concatenate(row_sums), core, x)
            small = jnp.concatenate(head_sums + [kept.reshape(-1)])
            terms = weight_grads(ffn_pairs, owners, extra_rows(small, 2 * ffn_half))
            final = ARRIVAL[-1]
            attn_chunks[final], terms = tie((attn_chunks[final], terms))
            joint = sum_owners(terms)
        grad_q = {}
        grad_k, grad_v = jnp.zeros(keys.shape, F32), jnp.zeros(keys.shape, F32)
        for hop in ARRIVAL:
            grad_q[hop], grad_k, grad_v = attend_back(
                attn_chunks[hop], out_mat, qkv[hop][0], keys, values, soft[hop], grad_k, grad_v
            )
        parts, grad_qkv, sums = {}, {}, []
        for hop in ORDER:
            grad_qkv[hop], qkv_sum, *parts[hop] = inputs_back(
                grad_q[hop], grad_k, grad_v, HOPS.index(hop), qkv_mat
            )
            sums.append(qkv_sum[0])
        grad_rows = grad_first + scatter_pairs(parts)
        bias_terms = sum(sums)
        pair_sums = jnp.concatenate([bias_terms[:head_cols], bias_terms[2 * head_cols :]])
        attn_pairs = [(inputs, grad_qkv), (attn_chunks, attended)]
        if layer:
            head_sums.append(pair_sums)
            terms = weight_grads(attn_pairs, owners)
            grad_rows, terms, found = tie((grad_rows, terms, found))
            ffn_grads[layer] = swap_core_z(found.astype(BF16))
            pending = sum_owners(terms)
        else:
            terms = weight_grads(attn_pairs, owners, extra_rows(pair_sums, attn_cols))
            terms, joint = tie((terms, joint))
            last = lax.all_to_all(terms, OWNERS, 0, 0, tiled=True)
    ffn_grads[0] = swap_core_z(joint[:shard_rows].astype(BF16))
    early_sums = joint[shard_rows:].reshape(-1)[: small.shape[0]]

    head_len = sum(item.shape[0] for item in head_sums)
    piece = early_sums[head_len:].reshape(layers * 6, -1)
    table = jnp.zeros((2, ring) + piece.shape, F32)
    for hop in HOPS:
        one = along_x(piece, hop) if hop else piece
        where = lax.rem(x + ring - hop, ring)
        table = lax.dynamic_update_slice(table, one[None, None], (core, where, 0, 0))
    pair = lax.dynamic_slice_in_dim(table, core, 1, 0)
    table = lax.dynamic_update_slice(table, other_core(pair), (1 - core, 0, 0, 0))
    rows_out = jnp.transpose(table, (2, 0, 1, 3)).reshape(layers, 6, -1)[::-1]

    def cols(pieces, start, count, turn=False):
        chosen = [piece[:, start : start + count].astype(F32) for piece in pieces]
        return jnp.stack([jnp.swapaxes(one, 0, 1) if turn else one for one in chosen])

    ups, pairs, place = [None] * layers, [None] * layers, 0
    for layer in reversed(range(layers)):
        ups[layer] = early_sums[place : place + ffn_half]
        place += ffn_half
        if layer:
            pairs[layer] = early_sums[place : place + 2 * head_cols]
            place += 2 * head_cols
    done = (
        layer_output,
        cols(ffn_grads, 0, ffn_half),
        cols(ffn_grads, ffn_half, ffn_half, True),
        swap_core_z(jnp.stack(ups)),
        [rows_out[:, index] for index in range(6)],
    )
    last, done = tie((last, done))
    layer_output, up_grads, down_grads, up_all, row_grads = done
    got = jnp.sum(last.astype(F32), axis=0)
    attn_grads[0] = swap_core_z(got[:shard_rows].astype(BF16))
    pairs[0] = got[shard_rows:].reshape(-1)[: 2 * head_cols]
    pair_all = swap_core_z(jnp.stack(pairs))
    input_grad = swap_core_z(grad_rows.astype(BF16)).astype(F32)

    return (
        layer_output,
        input_grad,
        cols(attn_grads, 0, head_cols),
        cols(attn_grads, head_cols, head_cols),
        cols(attn_grads, 2 * head_cols, head_cols),
        cols(attn_grads, qkv_cols, head_cols, True),
        up_grads,
        down_grads,
        pair_all[:, :head_cols],
        pair_all[:, head_cols:],
        up_all,
        *row_grads,
    )


def solution(mesh):
    split = Mesh(mesh.devices.reshape(4, 2, 2, 2, 4), AXES)
    rows = P(DP + TENSOR, None)
    tall = P(None, DP, TENSOR)
    wide = P(None, TENSOR, DP)
    held = P(None, TENSOR)
    return jax.shard_map(
        on_device,
        mesh=split,
        in_specs=(rows, rows, P(DP), P(DP), tall, tall, tall, wide, tall, wide, held, held, held)
        + (P(),) * 6,
        out_specs=(rows, rows, tall, tall, tall, wide, tall, wide, held, held, held) + (P(),) * 6,
        check_vma=False,
    )
```

```python
import jax
import jax.numpy as jnp
from jax import lax
from jax.experimental import pallas as pl
from jax.experimental.pallas import tpu as pltpu
from jax.sharding import Mesh, PartitionSpec as P

HEAD_DIM = 64
NORM_EPS = 1e-12
MASKED = -1000000000.0
F32 = jnp.float32
BF16 = jnp.bfloat16

AXES = ("y", "zl", "c", "zh", "x")
DP = ("y", "zl", "c")
TENSOR = ("zh", "x")
OWNERS = ("y", "zl", "zh")
HOPS = (0, 1, 3, 2)
ORDER = (2, 1, 3, 0)
ARRIVAL = (0, 1, 3, 2)


def dot(left, right, left_dim, right_dim):
    return lax.dot_general(
        left, right, (((left_dim,), (right_dim,)), ((), ())), preferred_element_type=F32
    )


def along_x(value, hop):
    ring = lax.axis_size("x")
    return lax.ppermute(value, "x", [(i, (i + hop) % ring) for i in range(ring)])


def other_core(value):
    return lax.ppermute(value, "c", [(0, 1), (1, 0)])


def swap_core_z(value):
    ring = lax.axis_size("x")
    pairs = []
    for core in range(2):
        for high in range(2):
            for x in range(ring):
                pairs.append(((core * 2 + high) * ring + x, (high * 2 + core) * ring + x))
    return lax.ppermute(value, ("c", "zh", "x"), pairs)


def gather_pairs(rows):
    mine = {hop: along_x(rows, hop) if hop else rows for hop in (1, 3, 2, 0)}
    return {hop: (mine[hop], other_core(mine[hop])) for hop in ARRIVAL}


def scatter_pairs(parts):
    total = None
    for hop in ORDER:
        keep, send = parts[hop]
        both = keep + other_core(send).astype(F32)
        if hop:
            both = along_x(both.astype(BF16), -hop).astype(F32)
        total = both if total is None else total + both
    return total


def normalized(rows):
    center = rows - jnp.mean(rows, axis=-1, keepdims=True)
    spread = jnp.mean(center * center, axis=-1, keepdims=True)
    scale = lax.rsqrt(spread + NORM_EPS)
    return center * scale, scale


def norm_back(grad, unit, scale, gain):
    gain_grad = jnp.sum(grad * unit, axis=0)
    shift_grad = jnp.sum(grad, axis=0)
    scaled = grad * gain
    mean_all = jnp.mean(scaled, axis=-1, keepdims=True)
    mean_unit = jnp.mean(scaled * unit, axis=-1, keepdims=True)
    return scale * (scaled - mean_all - unit * mean_unit), gain_grad, shift_grad


def whole(array):
    rank = len(array.shape)
    return pl.BlockSpec(array.shape, lambda *_: (0,) * rank)


def call(body, args, outs, flops, grid=(), in_specs=None, out_specs=None, room=40):
    size = sum(a.size * a.dtype.itemsize for a in (*args, *outs))
    return pl.pallas_call(
        body,
        grid=grid,
        in_specs=in_specs or [whole(a) for a in args],
        out_specs=out_specs or [whole(o) for o in outs],
        out_shape=list(outs),
        compiler_params=pltpu.CompilerParams(vmem_limit_bytes=room * 1024 * 1024),
        cost_estimate=pl.CostEstimate(flops=flops, bytes_accessed=size, transcendentals=0),
    )(*args)


def shaped(shape, dtype):
    return jax.ShapeDtypeStruct(shape, dtype)


def both_rows(mine, other):
    return jnp.concatenate([mine[...], other[...]], axis=0)


def store_part(part, keep, send):
    half = keep.shape[0]
    keep[...] = part[:half]
    send[...] = part[half:].astype(BF16)


def part_shapes(rows, width):
    return [shaped((rows, width), F32), shaped((rows, width), BF16)]


def qkv_body(mine, other, mat, bias, query, key, value):
    out = (dot(both_rows(mine, other), mat[...], 1, 0) + bias[...]).astype(BF16)
    step = query.shape[1]
    query[...] = out[:, :step]
    key[...] = out[:, step : 2 * step]
    value[...] = out[:, 2 * step :]


def make_qkv(pair, mat, bias):
    rows, width = pair[0].shape
    out = shaped((2 * rows, mat.shape[1] // 3), BF16)
    return call(qkv_body, (*pair, mat, bias), [out] * 3, 4 * rows * mat.size)


def lanes_of(shape, head):
    return lax.broadcasted_iota(jnp.int32, shape, 1) // HEAD_DIM == head


def attend_body(query, key, value, row_mark, key_mark, out_mat, mixed, soft, keep, send):
    allowed = row_mark[...] == key_mark[...]
    total = jnp.zeros(query.shape, F32)
    for head in range(soft.shape[0]):
        lanes = lanes_of(query.shape, head)
        chosen = jnp.where(lanes, query[...], jnp.zeros(query.shape, BF16))
        scores = dot(chosen, key[...], 1, 1) * HEAD_DIM**-0.5
        scores = jnp.where(allowed, scores, MASKED)
        exps = jnp.exp(scores - jnp.max(scores, axis=-1, keepdims=True))
        probs = (exps * (1.0 / jnp.sum(exps, axis=-1, keepdims=True))).astype(BF16)
        soft[head] = probs
        total = jnp.where(lanes, dot(probs, value[...], 1, 0), total)
    low = total.astype(BF16)
    mixed[...] = low
    store_part(dot(low, out_mat[...], 1, 1), keep, send)


def attend(query, key, value, row_mark, key_mark, out_mat):
    rows, width = query.shape
    heads = width // HEAD_DIM
    outs = [shaped((rows, width), BF16), shaped((heads, rows, key.shape[0]), BF16)]
    outs += part_shapes(rows // 2, out_mat.shape[0])
    flops = 4 * heads * rows * key.size + 2 * rows * out_mat.size
    return call(attend_body, (query, key, value, row_mark, key_mark, out_mat), outs, 3 * flops)


def attend_back_body(mine, other, out_mat, query, key, value, soft, key_in, value_in, grad_query, key_out, value_out):
    grads = dot(both_rows(mine, other), out_mat[...], 1, 0).astype(BF16)
    for_query = jnp.zeros(query.shape, F32)
    for_key = jnp.zeros(key.shape, F32)
    for_value = jnp.zeros(key.shape, F32)
    for head in range(soft.shape[0]):
        lanes = lanes_of(query.shape, head)
        tall = lanes_of(key.shape, head)
        probs = soft[head]
        wide = probs.astype(F32)
        chosen = jnp.where(lanes, grads, jnp.zeros(query.shape, BF16))
        grad_soft = dot(chosen, value[...], 1, 1)
        row = jnp.sum(grad_soft * wide, axis=-1, keepdims=True)
        scores = (wide * (grad_soft - row)).astype(BF16)
        for_query = jnp.where(lanes, dot(scores, key[...], 1, 0), for_query)
        for_key = jnp.where(tall, dot(scores, query[...], 0, 0), for_key)
        for_value = jnp.where(tall, dot(probs, grads, 0, 0), for_value)
    grad_query[...] = (for_query * HEAD_DIM**-0.5).astype(BF16)
    key_out[...] = key_in[...] + for_key * HEAD_DIM**-0.5
    value_out[...] = value_in[...] + for_value


def attend_back(pair, out_mat, query, key, value, soft, key_sum, value_sum):
    outs = [shaped(query.shape, BF16), shaped(key.shape, F32), shaped(key.shape, F32)]
    args = (*pair, out_mat, query, key, value, soft, key_sum, value_sum)
    flops = 8 * soft.shape[0] * query.shape[0] * key.size
    half = pl.BlockSpec((query.shape[0] // 2, pair[0].shape[1]), lambda *_: (0, 0))
    specs = [half, half] + [whole(a) for a in args[2:]]
    return call(attend_back_body, args, outs, 2 * flops, (1,), specs)


def inputs_back_body(grad_query, grad_key, grad_value, mat, joined, sums, keep, send):
    rows = jnp.concatenate(
        [grad_query[...], grad_key[...].astype(BF16), grad_value[...].astype(BF16)], axis=1
    )
    joined[...] = rows
    sums[...] = jnp.sum(rows.astype(F32), axis=0, keepdims=True)
    store_part(dot(rows, mat[...], 1, 1), keep, send)


def inputs_back(grad_query, grad_key, grad_value, index, mat):
    rows, width = grad_query.shape
    outs = [shaped((rows, 3 * width), BF16), shaped((1, 3 * width), F32)]
    outs += part_shapes(rows // 2, mat.shape[0])
    block = pl.BlockSpec((rows, width), lambda *_: (index, 0))
    args = (grad_query, grad_key, grad_value, mat)
    specs = [whole(grad_query), block, block, whole(mat)]
    return call(inputs_back_body, args, outs, 2 * rows * mat.size, (1,), specs)


def ffn_body(mine, other, up, bias, down, act, slope, keep, send):
    pre = dot(both_rows(mine, other), up[...], 1, 0) + bias[...]
    area = 0.5 + 0.5 * lax.erf(pre * 0.7071067811865476)
    low = (pre * area).astype(BF16)
    act[...] = low
    slope[...] = (area + pre * (jnp.exp(pre * pre * -0.5) * 0.3989422804014327)).astype(BF16)
    store_part(dot(low, down[...], 1, 1), keep, send)


def ffn(pair, up, bias, down):
    rows, width = pair[0].shape
    outs = [shaped((2 * rows, up.shape[1]), BF16)] * 2 + part_shapes(rows, width)
    return call(ffn_body, (*pair, up, bias, down), outs, 4 * rows * (up.size + down.size))


def ffn_back_body(mine, other, up, down, slope, grad, sums, keep, send):
    low = (dot(both_rows(mine, other), down[...], 1, 0) * slope[...].astype(F32)).astype(BF16)
    grad[...] = low
    sums[...] = jnp.sum(low.astype(F32), axis=0, keepdims=True)
    store_part(dot(low, up[...], 1, 1), keep, send)


def ffn_back(pair, up, down, slope):
    rows, width = pair[0].shape
    outs = [shaped(slope.shape, BF16), shaped((1, slope.shape[1]), F32)] + part_shapes(rows, width)
    return call(ffn_back_body, (*pair, up, down, slope), outs, 4 * rows * (up.size + down.size))


def weight_grads(pairs, owners, extra=None):
    count = len(HOPS)
    tile = 256
    args, specs, cols = [], [], 0
    for left, right in pairs:
        flat = [half for hop in HOPS for half in left[hop]]
        rows, width = right[0].shape[0] // 2, flat[0].shape[1]
        args += flat + [right[hop] for hop in HOPS]
        specs += [pl.BlockSpec((rows, tile), lambda i: (0, i))] * len(flat)
        specs += [whole(right[hop]) for hop in HOPS]
        cols += right[0].shape[1]
    slab = width // owners
    depth = slab
    if extra is not None:
        args.append(extra)
        specs.append(whole(extra))
        depth += extra.shape[0]

    def body(*refs):
        out = refs[-1]
        start = 0
        for index in range(len(pairs)):
            here = refs[index * 3 * count : (index + 1) * 3 * count]
            left = jnp.concatenate([ref[...] for ref in here[: 2 * count]], axis=0)
            right = jnp.concatenate([ref[...] for ref in here[2 * count :]], axis=0)
            end = start + right.shape[1]
            found = dot(left, right, 0, 0).astype(BF16)
            for part in range(tile // slab):
                out[part, :slab, start:end] = found[part * slab : (part + 1) * slab]
            start = end
        if extra is not None:
            for part in range(tile // slab):
                out[part, slab:, :] = refs[-2][...]

    out = shaped((owners, depth, cols), BF16)
    out_spec = pl.BlockSpec((tile // slab, depth, cols), lambda i: (i, 0, 0))
    flops = 2 * rows * 2 * count * width * cols
    return call(body, args, [out], 2 * flops, (width // tile,), specs, [out_spec], 58)[0]


def stack_chunks(chunks):
    return jnp.concatenate([chunks[hop] for hop in HOPS], axis=0)


def sum_rows(chunks, start, count, core, x):
    ring = lax.axis_size("x")
    table = [[chunks[hop][side][start : start + 2 * count] for hop in range(ring)] for side in (0, 1)]
    table = jnp.stack([jnp.stack(side) for side in table]).astype(F32)
    table = jnp.where(core == 0, table, table[::-1])
    ordered = [
        lax.dynamic_index_in_dim(table, lax.rem(x + ring - where, ring), 1, False)
        for where in range(ring)
    ]
    total = jnp.sum(jnp.stack(ordered), axis=(0, 1))
    return total[:count] + total[count:]


def on_device(
    layer_input,
    cotangent,
    segment,
    live_mask,
    query_weight,
    key_weight,
    value_weight,
    out_weight,
    up_weight,
    down_weight,
    query_bias,
    value_bias,
    up_bias,
    out_bias,
    down_bias,
    attention_gain,
    attention_shift,
    output_gain,
    output_shift,
):
    layers = query_weight.shape[0]
    core, high, x = lax.axis_index("c"), lax.axis_index("zh"), lax.axis_index("x")
    ring = lax.axis_size("x")
    owners = 16
    rows_in = swap_core_z(layer_input)

    head_cols = query_weight.shape[2]
    qkv_cols = 3 * head_cols
    shard_rows = query_weight.shape[1]
    ffn_half = up_weight.shape[2]
    qkv_shards = jnp.concatenate([query_weight, key_weight, value_weight], axis=2)

    turned_out = jnp.swapaxes(out_weight, 1, 2)
    first = swap_core_z(jnp.concatenate([qkv_shards[0], turned_out[0]], axis=1))
    spread = jnp.broadcast_to(first, (owners,) + first.shape)
    first = lax.all_to_all(spread, OWNERS, 0, 0, tiled=True).reshape(-1, first.shape[1])

    def gather_mat(*shards):
        mat = lax.all_gather(jnp.concatenate(shards, axis=1), DP, axis=0, tiled=True)
        return swap_core_z(mat)

    attn_mats, ffn_mats = [], []
    for layer in range(layers):
        if layer:
            attn_mats.append(gather_mat(qkv_shards[layer], turned_out[layer]))
        else:
            attn_mats.append(first)
        ffn_mats.append(gather_mat(up_weight[layer], jnp.swapaxes(down_weight[layer], 0, 1)))
    qkv_mats = [mat[:, :qkv_cols] for mat in attn_mats]
    out_mats = [mat[:, qkv_cols:] for mat in attn_mats]
    up_mats = [mat[:, :ffn_half] for mat in ffn_mats]
    down_mats = [mat[:, ffn_half:] for mat in ffn_mats]

    biases = jnp.concatenate([query_bias, value_bias, up_bias], axis=1)
    biases = swap_core_z(biases)
    query_bias = biases[:, :head_cols]
    value_bias = biases[:, head_cols : 2 * head_cols]
    up_bias = biases[:, 2 * head_cols :]

    packed = (segment * 2 + live_mask).astype(F32)
    packed = jnp.where(core == high, packed, other_core(packed)).reshape(2, ring, -1)
    packed = jnp.where(core == 0, packed, packed[::-1])
    ordered = []
    for hop in HOPS:
        ordered.append(lax.dynamic_index_in_dim(packed, lax.rem(x + ring - hop, ring), 1, False))
    marks = jnp.stack(ordered).reshape(len(HOPS), -1)
    seg_chunks = jnp.floor(marks * 0.5)
    live = (marks - 2 * seg_chunks).reshape(-1)
    key_mark = jnp.where(live > 0.5, seg_chunks.reshape(-1), -1.0)
    row_marks = {hop: seg_chunks[index][:, None] for index, hop in enumerate(HOPS)}
    key_mark = key_mark[None, :]

    current = rows_in.astype(F32)
    saved = []
    for layer in range(layers):
        qkv_mat, out_mat = qkv_mats[layer], out_mats[layer]
        up_mat, down_mat = up_mats[layer], down_mats[layer]
        qkv_bias = jnp.concatenate(
            [query_bias[layer], jnp.zeros_like(query_bias[layer]), value_bias[layer]]
        )
        inputs = gather_pairs(current.astype(BF16))
        qkv = {hop: make_qkv(inputs[hop], qkv_mat, qkv_bias[None, :]) for hop in ARRIVAL}
        keys = stack_chunks({hop: qkv[hop][1] for hop in HOPS})
        values = stack_chunks({hop: qkv[hop][2] for hop in HOPS})
        attended, soft, parts = {}, {}, {}
        for hop in ORDER:
            attended[hop], soft[hop], *parts[hop] = attend(
                qkv[hop][0], keys, values, row_marks[hop], key_mark, out_mat
            )
        first_sum = current + scatter_pairs(parts) + out_bias[layer]
        mid_unit, mid_scale = normalized(first_sum)
        normed_mid = mid_unit * attention_gain[layer] + attention_shift[layer]
        mids = gather_pairs(normed_mid.astype(BF16))
        activated, slopes, parts = {}, {}, {}
        for hop in ARRIVAL:
            activated[hop], slopes[hop], *parts[hop] = ffn(
                mids[hop], up_mat, up_bias[layer][None, :], down_mat
            )
        second_sum = normed_mid + scatter_pairs(parts) + down_bias[layer]
        out_unit, out_scale = normalized(second_sum)
        current = out_unit * output_gain[layer] + output_shift[layer]
        saved.append(
            (inputs, qkv, keys, values, attended, soft, mid_unit, mid_scale, mids, slopes,
             activated, out_unit, out_scale)
        )
    layer_output = swap_core_z(current.astype(BF16)).astype(F32)

    grad_rows = swap_core_z(cotangent).astype(F32)
    attn_cols = qkv_cols + head_cols

    def sum_owners(terms):
        return jnp.sum(lax.all_to_all(terms, OWNERS, 0, 0, tiled=True).astype(F32), axis=0)

    def extra_rows(values, cols):
        count = -(-values.shape[0] // (16 * cols)) * 16
        padded = jnp.pad(values, (0, count * cols - values.shape[0]))
        return padded.reshape(count, cols).astype(BF16)

    ffn_grads, attn_grads = [None] * layers, [None] * layers
    row_sums, head_sums, pending = [], [], None
    tie = lax.optimization_barrier
    for layer in reversed(range(layers)):
        (inputs, qkv, keys, values, attended, soft, mid_unit, mid_scale, mids, slopes,
         activated, out_unit, out_scale) = saved[layer]
        qkv_mat, out_mat = qkv_mats[layer], out_mats[layer]
        up_mat, down_mat = up_mats[layer], down_mats[layer]
        grad_second, out_gain_term, out_shift_term = norm_back(
            grad_rows, out_unit, out_scale, output_gain[layer]
        )
        branch_low = grad_second.astype(BF16)
        down_bias_term = jnp.sum(branch_low.astype(F32), axis=0)
        branch = gather_pairs(branch_low)
        grad_pre, parts, up_sums = {}, {}, []
        for hop in ARRIVAL:
            grad_pre[hop], up_sum, *parts[hop] = ffn_back(
                branch[hop], up_mat, down_mat, slopes[hop]
            )
            up_sums.append(up_sum[0])
        grad_mid = grad_second + scatter_pairs(parts)
        up_bias_term = sum(up_sums)
        ffn_pairs = [(mids, grad_pre), (branch, activated)]
        if layer:
            grad_mid, terms = tie((grad_mid, weight_grads(ffn_pairs, owners)))
            found = sum_owners(terms)
        if pending is not None:
            grad_mid, pending = tie((grad_mid, pending))
            attn_grads[layer + 1] = swap_core_z(pending.astype(BF16))
        grad_first, att_gain_term, att_shift_term = norm_back(
            grad_mid, mid_unit, mid_scale, attention_gain[layer]
        )
        attn_low = grad_first.astype(BF16)
        out_bias_term = jnp.sum(attn_low.astype(F32), axis=0)
        own_sums = jnp.stack(
            [out_bias_term, down_bias_term, att_gain_term, att_shift_term, out_gain_term,
             out_shift_term]
        )
        upper = own_sums.astype(BF16)
        lower = (own_sums - upper.astype(F32)).astype(BF16)
        blank = jnp.zeros((16 - 2 * upper.shape[0], upper.shape[1]), BF16)
        block = tie(jnp.concatenate([attn_low, upper, lower, blank], axis=0))
        attn_chunks = gather_pairs(block)
        row_sums.append(sum_rows(attn_chunks, attn_low.shape[0], upper.shape[0], core, x))
        head_sums.append(up_bias_term)
        if not layer:
            small = jnp.concatenate(head_sums + [item.reshape(-1) for item in row_sums])
            terms = weight_grads(ffn_pairs, owners, extra_rows(small, 2 * ffn_half))
            final = ARRIVAL[-1]
            attn_chunks[final], terms = tie((attn_chunks[final], terms))
            joint = sum_owners(terms)
        grad_q = {}
        grad_k, grad_v = jnp.zeros(keys.shape, F32), jnp.zeros(keys.shape, F32)
        for hop in ARRIVAL:
            grad_q[hop], grad_k, grad_v = attend_back(
                attn_chunks[hop], out_mat, qkv[hop][0], keys, values, soft[hop], grad_k, grad_v
            )
        parts, grad_qkv, sums = {}, {}, []
        for hop in ORDER:
            grad_qkv[hop], qkv_sum, *parts[hop] = inputs_back(
                grad_q[hop], grad_k, grad_v, HOPS.index(hop), qkv_mat
            )
            sums.append(qkv_sum[0])
        grad_rows = grad_first + scatter_pairs(parts)
        bias_terms = sum(sums)
        pair_sums = jnp.concatenate([bias_terms[:head_cols], bias_terms[2 * head_cols :]])
        attn_pairs = [(inputs, grad_qkv), (attn_chunks, attended)]
        if layer:
            head_sums.append(pair_sums)
            terms = weight_grads(attn_pairs, owners)
            grad_rows, terms, found = tie((grad_rows, terms, found))
            ffn_grads[layer] = swap_core_z(found.astype(BF16))
            pending = sum_owners(terms)
        else:
            terms = weight_grads(attn_pairs, owners, extra_rows(pair_sums, attn_cols))
            terms, joint = tie((terms, joint))
            last = lax.all_to_all(terms, OWNERS, 0, 0, tiled=True)
    ffn_grads[0] = swap_core_z(joint[:shard_rows].astype(BF16))
    early_sums = joint[shard_rows:].reshape(-1)[: small.shape[0]]

    head_len = sum(item.shape[0] for item in head_sums)
    rows_out = early_sums[head_len:].reshape(layers, 6, -1)[::-1]

    def cols(pieces, start, count, turn=False):
        chosen = [piece[:, start : start + count].astype(F32) for piece in pieces]
        return jnp.stack([jnp.swapaxes(one, 0, 1) if turn else one for one in chosen])

    ups, pairs, place = [None] * layers, [None] * layers, 0
    for layer in reversed(range(layers)):
        ups[layer] = early_sums[place : place + ffn_half]
        place += ffn_half
        if layer:
            pairs[layer] = early_sums[place : place + 2 * head_cols]
            place += 2 * head_cols
    done = (
        layer_output,
        cols(ffn_grads, 0, ffn_half),
        cols(ffn_grads, ffn_half, ffn_half, True),
        swap_core_z(jnp.stack(ups)),
        [rows_out[:, index] for index in range(6)],
    )
    last, done = tie((last, done))
    layer_output, up_grads, down_grads, up_all, row_grads = done
    got = jnp.sum(last.astype(F32), axis=0)
    attn_grads[0] = swap_core_z(got[:shard_rows].astype(BF16))
    pairs[0] = got[shard_rows:].reshape(-1)[: 2 * head_cols]
    pair_all = swap_core_z(jnp.stack(pairs))
    input_grad = swap_core_z(grad_rows.astype(BF16)).astype(F32)

    return (
        layer_output,
        input_grad,
        cols(attn_grads, 0, head_cols),
        cols(attn_grads, head_cols, head_cols),
        cols(attn_grads, 2 * head_cols, head_cols),
        cols(attn_grads, qkv_cols, head_cols, True),
        up_grads,
        down_grads,
        pair_all[:, :head_cols],
        pair_all[:, head_cols:],
        up_all,
        *row_grads,
    )


def solution(mesh):
    split = Mesh(mesh.devices.reshape(4, 2, 2, 2, 4), AXES)
    rows = P(DP + TENSOR, None)
    tall = P(None, DP, TENSOR)
    wide = P(None, TENSOR, DP)
    held = P(None, TENSOR)
    return jax.shard_map(
        on_device,
        mesh=split,
        in_specs=(rows, rows, P(DP), P(DP), tall, tall, tall, wide, tall, wide, held, held, held)
        + (P(),) * 6,
        out_specs=(rows, rows, tall, tall, tall, wide, tall, wide, held, held, held) + (P(),) * 6,
        check_vma=False,
    )
```

```python
import jax
import jax.numpy as jnp
from jax import lax
from jax.experimental import pallas as pl
from jax.experimental.pallas import tpu as pltpu
from jax.sharding import Mesh, PartitionSpec as P

HEAD_DIM = 64
NORM_EPS = 1e-12
MASKED = -1000000000.0
F32 = jnp.float32
BF16 = jnp.bfloat16

AXES = ("y", "zl", "c", "zh", "x")
DP = ("y", "zl", "c")
TENSOR = ("zh", "x")
OWNERS = ("y", "zl", "zh")
HOPS = (0, 1, 3, 2)
ORDER = (2, 1, 3, 0)
ARRIVAL = (0, 1, 3, 2)


def dot(left, right, left_dim, right_dim):
    return lax.dot_general(
        left, right, (((left_dim,), (right_dim,)), ((), ())), preferred_element_type=F32
    )


def along_x(value, hop):
    ring = lax.axis_size("x")
    return lax.ppermute(value, "x", [(i, (i + hop) % ring) for i in range(ring)])


def other_core(value):
    return lax.ppermute(value, "c", [(0, 1), (1, 0)])


def swap_core_z(value):
    ring = lax.axis_size("x")
    pairs = []
    for core in range(2):
        for high in range(2):
            for x in range(ring):
                pairs.append(((core * 2 + high) * ring + x, (high * 2 + core) * ring + x))
    return lax.ppermute(value, ("c", "zh", "x"), pairs)


def gather_pairs(rows):
    mine = {hop: along_x(rows, hop) if hop else rows for hop in (1, 3, 2, 0)}
    return {hop: (mine[hop], other_core(mine[hop])) for hop in ARRIVAL}


def scatter_pairs(parts):
    total = None
    for hop in ORDER:
        keep, send = parts[hop]
        both = keep + other_core(send).astype(F32)
        if hop:
            both = along_x(both.astype(BF16), -hop).astype(F32)
        total = both if total is None else total + both
    return total


def normalized(rows):
    center = rows - jnp.mean(rows, axis=-1, keepdims=True)
    spread = jnp.mean(center * center, axis=-1, keepdims=True)
    scale = lax.rsqrt(spread + NORM_EPS)
    return center * scale, scale


def norm_back(grad, unit, scale, gain):
    gain_grad = jnp.sum(grad * unit, axis=0)
    shift_grad = jnp.sum(grad, axis=0)
    scaled = grad * gain
    mean_all = jnp.mean(scaled, axis=-1, keepdims=True)
    mean_unit = jnp.mean(scaled * unit, axis=-1, keepdims=True)
    return scale * (scaled - mean_all - unit * mean_unit), gain_grad, shift_grad


def whole(array):
    rank = len(array.shape)
    return pl.BlockSpec(array.shape, lambda *_: (0,) * rank)


def call(body, args, outs, flops, grid=(), in_specs=None, out_specs=None, room=40):
    size = sum(a.size * a.dtype.itemsize for a in (*args, *outs))
    return pl.pallas_call(
        body,
        grid=grid,
        in_specs=in_specs or [whole(a) for a in args],
        out_specs=out_specs or [whole(o) for o in outs],
        out_shape=list(outs),
        compiler_params=pltpu.CompilerParams(vmem_limit_bytes=room * 1024 * 1024),
        cost_estimate=pl.CostEstimate(flops=flops, bytes_accessed=size, transcendentals=0),
    )(*args)


def shaped(shape, dtype):
    return jax.ShapeDtypeStruct(shape, dtype)


def both_rows(mine, other):
    return jnp.concatenate([mine[...], other[...]], axis=0)


def store_part(part, keep, send):
    half = keep.shape[0]
    keep[...] = part[:half]
    send[...] = part[half:].astype(BF16)


def part_shapes(rows, width):
    return [shaped((rows, width), F32), shaped((rows, width), BF16)]


def qkv_body(mine, other, mat, bias, query, key, value):
    out = (dot(both_rows(mine, other), mat[...], 1, 0) + bias[...]).astype(BF16)
    step = query.shape[1]
    query[...] = out[:, :step]
    key[...] = out[:, step : 2 * step]
    value[...] = out[:, 2 * step :]


def make_qkv(pair, mat, bias):
    rows, width = pair[0].shape
    out = shaped((2 * rows, mat.shape[1] // 3), BF16)
    return call(qkv_body, (*pair, mat, bias), [out] * 3, 4 * rows * mat.size)


def lanes_of(shape, head):
    return lax.broadcasted_iota(jnp.int32, shape, 1) // HEAD_DIM == head


def attend_body(query, key, value, row_mark, key_mark, out_mat, mixed, soft, keep, send):
    allowed = row_mark[...] == key_mark[...]
    total = jnp.zeros(query.shape, F32)
    for head in range(soft.shape[0]):
        lanes = lanes_of(query.shape, head)
        chosen = jnp.where(lanes, query[...], jnp.zeros(query.shape, BF16))
        scores = dot(chosen, key[...], 1, 1) * HEAD_DIM**-0.5
        scores = jnp.where(allowed, scores, MASKED)
        exps = jnp.exp(scores - jnp.max(scores, axis=-1, keepdims=True))
        probs = (exps * (1.0 / jnp.sum(exps, axis=-1, keepdims=True))).astype(BF16)
        soft[head] = probs
        total = jnp.where(lanes, dot(probs, value[...], 1, 0), total)
    low = total.astype(BF16)
    mixed[...] = low
    store_part(dot(low, out_mat[...], 1, 1), keep, send)


def attend(query, key, value, row_mark, key_mark, out_mat):
    rows, width = query.shape
    heads = width // HEAD_DIM
    outs = [shaped((rows, width), BF16), shaped((heads, rows, key.shape[0]), BF16)]
    outs += part_shapes(rows // 2, out_mat.shape[0])
    flops = 4 * heads * rows * key.size + 2 * rows * out_mat.size
    return call(attend_body, (query, key, value, row_mark, key_mark, out_mat), outs, 3 * flops)


def attend_back_body(mine, other, out_mat, query, key, value, soft, key_in, value_in, grad_query, key_out, value_out):
    grads = dot(both_rows(mine, other), out_mat[...], 1, 0).astype(BF16)
    for_query = jnp.zeros(query.shape, F32)
    for_key = jnp.zeros(key.shape, F32)
    for_value = jnp.zeros(key.shape, F32)
    for head in range(soft.shape[0]):
        lanes = lanes_of(query.shape, head)
        tall = lanes_of(key.shape, head)
        probs = soft[head]
        wide = probs.astype(F32)
        chosen = jnp.where(lanes, grads, jnp.zeros(query.shape, BF16))
        grad_soft = dot(chosen, value[...], 1, 1)
        row = jnp.sum(grad_soft * wide, axis=-1, keepdims=True)
        scores = (wide * (grad_soft - row)).astype(BF16)
        for_query = jnp.where(lanes, dot(scores, key[...], 1, 0), for_query)
        for_key = jnp.where(tall, dot(scores, query[...], 0, 0), for_key)
        for_value = jnp.where(tall, dot(probs, grads, 0, 0), for_value)
    grad_query[...] = (for_query * HEAD_DIM**-0.5).astype(BF16)
    key_out[...] = key_in[...] + for_key * HEAD_DIM**-0.5
    value_out[...] = value_in[...] + for_value


def attend_back(pair, out_mat, query, key, value, soft, key_sum, value_sum):
    outs = [shaped(query.shape, BF16), shaped(key.shape, F32), shaped(key.shape, F32)]
    args = (*pair, out_mat, query, key, value, soft, key_sum, value_sum)
    flops = 8 * soft.shape[0] * query.shape[0] * key.size
    half = pl.BlockSpec((query.shape[0] // 2, pair[0].shape[1]), lambda *_: (0, 0))
    specs = [half, half] + [whole(a) for a in args[2:]]
    return call(attend_back_body, args, outs, 2 * flops, (1,), specs)


def inputs_back_body(grad_query, grad_key, grad_value, mat, joined, sums, keep, send):
    rows = jnp.concatenate(
        [grad_query[...], grad_key[...].astype(BF16), grad_value[...].astype(BF16)], axis=1
    )
    joined[...] = rows
    sums[...] = jnp.sum(rows.astype(F32), axis=0, keepdims=True)
    store_part(dot(rows, mat[...], 1, 1), keep, send)


def inputs_back(grad_query, grad_key, grad_value, index, mat):
    rows, width = grad_query.shape
    outs = [shaped((rows, 3 * width), BF16), shaped((1, 3 * width), F32)]
    outs += part_shapes(rows // 2, mat.shape[0])
    block = pl.BlockSpec((rows, width), lambda *_: (index, 0))
    args = (grad_query, grad_key, grad_value, mat)
    specs = [whole(grad_query), block, block, whole(mat)]
    return call(inputs_back_body, args, outs, 2 * rows * mat.size, (1,), specs)


def ffn_body(mine, other, up, bias, down, act, slope, keep, send):
    pre = dot(both_rows(mine, other), up[...], 1, 0) + bias[...]
    area = 0.5 + 0.5 * lax.erf(pre * 0.7071067811865476)
    low = (pre * area).astype(BF16)
    act[...] = low
    slope[...] = (area + pre * (jnp.exp(pre * pre * -0.5) * 0.3989422804014327)).astype(BF16)
    store_part(dot(low, down[...], 1, 1), keep, send)


def ffn(pair, up, bias, down):
    rows, width = pair[0].shape
    outs = [shaped((2 * rows, up.shape[1]), BF16)] * 2 + part_shapes(rows, width)
    return call(ffn_body, (*pair, up, bias, down), outs, 4 * rows * (up.size + down.size))


def ffn_back_body(mine, other, up, down, slope, grad, sums, keep, send):
    low = (dot(both_rows(mine, other), down[...], 1, 0) * slope[...].astype(F32)).astype(BF16)
    grad[...] = low
    sums[...] = jnp.sum(low.astype(F32), axis=0, keepdims=True)
    store_part(dot(low, up[...], 1, 1), keep, send)


def ffn_back(pair, up, down, slope):
    rows, width = pair[0].shape
    outs = [shaped(slope.shape, BF16), shaped((1, slope.shape[1]), F32)] + part_shapes(rows, width)
    return call(ffn_back_body, (*pair, up, down, slope), outs, 4 * rows * (up.size + down.size))


def weight_grads(pairs, owners, extra=None):
    count = len(HOPS)
    tile = 256
    args, specs, cols = [], [], 0
    for left, right in pairs:
        flat = [half for hop in HOPS for half in left[hop]]
        rows, width = right[0].shape[0] // 2, flat[0].shape[1]
        args += flat + [right[hop] for hop in HOPS]
        specs += [pl.BlockSpec((rows, tile), lambda i: (0, i))] * len(flat)
        specs += [whole(right[hop]) for hop in HOPS]
        cols += right[0].shape[1]
    slab = width // owners
    depth = slab
    if extra is not None:
        args.append(extra)
        specs.append(whole(extra))
        depth += extra.shape[0]

    def body(*refs):
        out = refs[-1]
        start = 0
        for index in range(len(pairs)):
            here = refs[index * 3 * count : (index + 1) * 3 * count]
            left = jnp.concatenate([ref[...] for ref in here[: 2 * count]], axis=0)
            right = jnp.concatenate([ref[...] for ref in here[2 * count :]], axis=0)
            end = start + right.shape[1]
            found = dot(left, right, 0, 0).astype(BF16)
            for part in range(tile // slab):
                out[part, :slab, start:end] = found[part * slab : (part + 1) * slab]
            start = end
        if extra is not None:
            for part in range(tile // slab):
                out[part, slab:, :] = refs[-2][...]

    out = shaped((owners, depth, cols), BF16)
    out_spec = pl.BlockSpec((tile // slab, depth, cols), lambda i: (i, 0, 0))
    flops = 2 * rows * 2 * count * width * cols
    return call(body, args, [out], 2 * flops, (width // tile,), specs, [out_spec], 58)[0]


def stack_chunks(chunks):
    return jnp.concatenate([chunks[hop] for hop in HOPS], axis=0)


def sum_rows(chunks, start, count, core, x):
    ring = lax.axis_size("x")
    table = [[chunks[hop][side][start : start + 2 * count] for hop in range(ring)] for side in (0, 1)]
    table = jnp.stack([jnp.stack(side) for side in table]).astype(F32)
    table = jnp.where(core == 0, table, table[::-1])
    ordered = [
        lax.dynamic_index_in_dim(table, lax.rem(x + ring - where, ring), 1, False)
        for where in range(ring)
    ]
    total = jnp.sum(jnp.stack(ordered), axis=(0, 1))
    return total[:count] + total[count:]


def on_device(
    layer_input,
    cotangent,
    segment,
    live_mask,
    query_weight,
    key_weight,
    value_weight,
    out_weight,
    up_weight,
    down_weight,
    query_bias,
    value_bias,
    up_bias,
    out_bias,
    down_bias,
    attention_gain,
    attention_shift,
    output_gain,
    output_shift,
):
    layers = query_weight.shape[0]
    core, high, x = lax.axis_index("c"), lax.axis_index("zh"), lax.axis_index("x")
    ring = lax.axis_size("x")
    owners = 16
    rows_in = swap_core_z(layer_input)

    head_cols = query_weight.shape[2]
    qkv_cols = 3 * head_cols
    shard_rows = query_weight.shape[1]
    ffn_half = up_weight.shape[2]
    qkv_shards = jnp.concatenate([query_weight, key_weight, value_weight], axis=2)

    turned_out = jnp.swapaxes(out_weight, 1, 2)
    first = swap_core_z(jnp.concatenate([qkv_shards[0], turned_out[0]], axis=1))
    spread = jnp.broadcast_to(first, (owners,) + first.shape)
    first = lax.all_to_all(spread, OWNERS, 0, 0, tiled=True).reshape(-1, first.shape[1])

    def gather_mat(*shards):
        mat = lax.all_gather(jnp.concatenate(shards, axis=1), DP, axis=0, tiled=True)
        return swap_core_z(mat)

    attn_mats, ffn_mats = [], []
    for layer in range(layers):
        if layer:
            attn_mats.append(gather_mat(qkv_shards[layer], turned_out[layer]))
        else:
            attn_mats.append(first)
        ffn_mats.append(gather_mat(up_weight[layer], jnp.swapaxes(down_weight[layer], 0, 1)))
    qkv_mats = [mat[:, :qkv_cols] for mat in attn_mats]
    out_mats = [mat[:, qkv_cols:] for mat in attn_mats]
    up_mats = [mat[:, :ffn_half] for mat in ffn_mats]
    down_mats = [mat[:, ffn_half:] for mat in ffn_mats]

    biases = jnp.concatenate([query_bias, value_bias, up_bias], axis=1)
    biases = swap_core_z(biases)
    query_bias = biases[:, :head_cols]
    value_bias = biases[:, head_cols : 2 * head_cols]
    up_bias = biases[:, 2 * head_cols :]

    packed = (segment * 2 + live_mask).astype(F32)
    packed = jnp.where(core == high, packed, other_core(packed)).reshape(2, ring, -1)
    packed = jnp.where(core == 0, packed, packed[::-1])
    ordered = []
    for hop in HOPS:
        ordered.append(lax.dynamic_index_in_dim(packed, lax.rem(x + ring - hop, ring), 1, False))
    marks = jnp.stack(ordered).reshape(len(HOPS), -1)
    seg_chunks = jnp.floor(marks * 0.5)
    live = (marks - 2 * seg_chunks).reshape(-1)
    key_mark = jnp.where(live > 0.5, seg_chunks.reshape(-1), -1.0)
    row_marks = {hop: seg_chunks[index][:, None] for index, hop in enumerate(HOPS)}
    key_mark = key_mark[None, :]

    current = rows_in.astype(F32)
    saved = []
    for layer in range(layers):
        qkv_mat, out_mat = qkv_mats[layer], out_mats[layer]
        up_mat, down_mat = up_mats[layer], down_mats[layer]
        qkv_bias = jnp.concatenate(
            [query_bias[layer], jnp.zeros_like(query_bias[layer]), value_bias[layer]]
        )
        inputs = gather_pairs(current.astype(BF16))
        qkv = {hop: make_qkv(inputs[hop], qkv_mat, qkv_bias[None, :]) for hop in ARRIVAL}
        keys = stack_chunks({hop: qkv[hop][1] for hop in HOPS})
        values = stack_chunks({hop: qkv[hop][2] for hop in HOPS})
        attended, soft, parts = {}, {}, {}
        for hop in ORDER:
            attended[hop], soft[hop], *parts[hop] = attend(
                qkv[hop][0], keys, values, row_marks[hop], key_mark, out_mat
            )
        first_sum = current + scatter_pairs(parts) + out_bias[layer]
        mid_unit, mid_scale = normalized(first_sum)
        normed_mid = mid_unit * attention_gain[layer] + attention_shift[layer]
        mids = gather_pairs(normed_mid.astype(BF16))
        activated, slopes, parts = {}, {}, {}
        for hop in ARRIVAL:
            activated[hop], slopes[hop], *parts[hop] = ffn(
                mids[hop], up_mat, up_bias[layer][None, :], down_mat
            )
        second_sum = normed_mid + scatter_pairs(parts) + down_bias[layer]
        out_unit, out_scale = normalized(second_sum)
        current = out_unit * output_gain[layer] + output_shift[layer]
        saved.append(
            (inputs, qkv, keys, values, attended, soft, mid_unit, mid_scale, mids, slopes,
             activated, out_unit, out_scale)
        )
    layer_output = swap_core_z(current.astype(BF16)).astype(F32)

    grad_rows = swap_core_z(cotangent).astype(F32)
    attn_cols = qkv_cols + head_cols

    def sum_owners(terms):
        return jnp.sum(lax.all_to_all(terms, OWNERS, 0, 0, tiled=True).astype(F32), axis=0)

    def extra_rows(values, cols):
        count = -(-values.shape[0] // (16 * cols)) * 16
        padded = jnp.pad(values, (0, count * cols - values.shape[0]))
        return padded.reshape(count, cols).astype(BF16)

    ffn_grads, attn_grads = [None] * layers, [None] * layers
    row_sums, head_sums, pending = [], [], None
    tie = lax.optimization_barrier
    for layer in reversed(range(layers)):
        (inputs, qkv, keys, values, attended, soft, mid_unit, mid_scale, mids, slopes,
         activated, out_unit, out_scale) = saved[layer]
        qkv_mat, out_mat = qkv_mats[layer], out_mats[layer]
        up_mat, down_mat = up_mats[layer], down_mats[layer]
        grad_second, out_gain_term, out_shift_term = norm_back(
            grad_rows, out_unit, out_scale, output_gain[layer]
        )
        branch_low = grad_second.astype(BF16)
        down_bias_term = jnp.sum(branch_low.astype(F32), axis=0)
        branch = gather_pairs(branch_low)
        grad_pre, parts, up_sums = {}, {}, []
        for hop in ARRIVAL:
            grad_pre[hop], up_sum, *parts[hop] = ffn_back(
                branch[hop], up_mat, down_mat, slopes[hop]
            )
            up_sums.append(up_sum[0])
        grad_mid = grad_second + scatter_pairs(parts)
        up_bias_term = sum(up_sums)
        ffn_pairs = [(mids, grad_pre), (branch, activated)]
        grad_first, att_gain_term, att_shift_term = norm_back(
            grad_mid, mid_unit, mid_scale, attention_gain[layer]
        )
        attn_low = grad_first.astype(BF16)
        out_bias_term = jnp.sum(attn_low.astype(F32), axis=0)
        own_sums = jnp.stack(
            [out_bias_term, down_bias_term, att_gain_term, att_shift_term, out_gain_term,
             out_shift_term]
        )
        upper = own_sums.astype(BF16)
        lower = (own_sums - upper.astype(F32)).astype(BF16)
        blank = jnp.zeros((16 - 2 * upper.shape[0], upper.shape[1]), BF16)
        block = tie(jnp.concatenate([attn_low, upper, lower, blank], axis=0))
        attn_chunks = gather_pairs(block)
        row_sums.append(sum_rows(attn_chunks, attn_low.shape[0], upper.shape[0], core, x))
        head_sums.append(up_bias_term)
        if not layer:
            small = jnp.concatenate(head_sums + [item.reshape(-1) for item in row_sums])
            terms = weight_grads(ffn_pairs, owners, extra_rows(small, 2 * ffn_half))
            final = ARRIVAL[-1]
            attn_chunks[final], terms, pending = tie((attn_chunks[final], terms, pending))
            pending = swap_core_z(pending.astype(BF16))
            ffn_grads[1] = pending[:, : 2 * ffn_half]
            attn_grads[1] = pending[:, 2 * ffn_half :]
            joint = sum_owners(terms)
        grad_q = {}
        grad_k, grad_v = jnp.zeros(keys.shape, F32), jnp.zeros(keys.shape, F32)
        for hop in ARRIVAL:
            grad_q[hop], grad_k, grad_v = attend_back(
                attn_chunks[hop], out_mat, qkv[hop][0], keys, values, soft[hop], grad_k, grad_v
            )
        parts, grad_qkv, sums = {}, {}, []
        for hop in ORDER:
            grad_qkv[hop], qkv_sum, *parts[hop] = inputs_back(
                grad_q[hop], grad_k, grad_v, HOPS.index(hop), qkv_mat
            )
            sums.append(qkv_sum[0])
        grad_rows = grad_first + scatter_pairs(parts)
        bias_terms = sum(sums)
        pair_sums = jnp.concatenate([bias_terms[:head_cols], bias_terms[2 * head_cols :]])
        attn_pairs = [(inputs, grad_qkv), (attn_chunks, attended)]
        if layer:
            head_sums.append(pair_sums)
            terms = weight_grads(ffn_pairs + attn_pairs, owners)
            grad_rows, terms = tie((grad_rows, terms))
            pending = sum_owners(terms)
        else:
            terms = weight_grads(attn_pairs, owners, extra_rows(pair_sums, attn_cols))
            terms, joint = tie((terms, joint))
            last = lax.all_to_all(terms, OWNERS, 0, 0, tiled=True)
    ffn_grads[0] = swap_core_z(joint[:shard_rows].astype(BF16))
    early_sums = joint[shard_rows:].reshape(-1)[: small.shape[0]]

    head_len = sum(item.shape[0] for item in head_sums)
    rows_out = early_sums[head_len:].reshape(layers, 6, -1)[::-1]

    def cols(pieces, start, count, turn=False):
        chosen = [piece[:, start : start + count].astype(F32) for piece in pieces]
        return jnp.stack([jnp.swapaxes(one, 0, 1) if turn else one for one in chosen])

    ups, pairs, place = [None] * layers, [None] * layers, 0
    for layer in reversed(range(layers)):
        ups[layer] = early_sums[place : place + ffn_half]
        place += ffn_half
        if layer:
            pairs[layer] = early_sums[place : place + 2 * head_cols]
            place += 2 * head_cols
    done = (
        layer_output,
        cols(ffn_grads, 0, ffn_half),
        cols(ffn_grads, ffn_half, ffn_half, True),
        swap_core_z(jnp.stack(ups)),
        [rows_out[:, index] for index in range(6)],
    )
    last, done = tie((last, done))
    layer_output, up_grads, down_grads, up_all, row_grads = done
    got = jnp.sum(last.astype(F32), axis=0)
    attn_grads[0] = swap_core_z(got[:shard_rows].astype(BF16))
    pairs[0] = got[shard_rows:].reshape(-1)[: 2 * head_cols]
    pair_all = swap_core_z(jnp.stack(pairs))
    input_grad = swap_core_z(grad_rows.astype(BF16)).astype(F32)

    return (
        layer_output,
        input_grad,
        cols(attn_grads, 0, head_cols),
        cols(attn_grads, head_cols, head_cols),
        cols(attn_grads, 2 * head_cols, head_cols),
        cols(attn_grads, qkv_cols, head_cols, True),
        up_grads,
        down_grads,
        pair_all[:, :head_cols],
        pair_all[:, head_cols:],
        up_all,
        *row_grads,
    )


def solution(mesh):
    split = Mesh(mesh.devices.reshape(4, 2, 2, 2, 4), AXES)
    rows = P(DP + TENSOR, None)
    tall = P(None, DP, TENSOR)
    wide = P(None, TENSOR, DP)
    held = P(None, TENSOR)
    return jax.shard_map(
        on_device,
        mesh=split,
        in_specs=(rows, rows, P(DP), P(DP), tall, tall, tall, wide, tall, wide, held, held, held)
        + (P(),) * 6,
        out_specs=(rows, rows, tall, tall, tall, wide, tall, wide, held, held, held) + (P(),) * 6,
        check_vma=False,
    )
```
